32 devices in a mesh: tile: 8 (over y, x, core), head: 4 (over z).
Axes of the slice: x: 2, y: 2, z: 4, core: 2. Of those that a mesh axis runs over, the one named last changes fastest.
Arguments:
- self_query: bfloat16 [1024, 5120], P('tile', 'head')
- self_key: bfloat16 [1024, 5120], P('tile', 'head')
- self_value: bfloat16 [1024, 5120], P('tile', 'head'), may hold values from -6 to 6
- cross_query: bfloat16 [1024, 5120], P('tile', 'head')
- text_key: bfloat16 [2048, 5120], P('tile', 'head'), as said below
- text_value: bfloat16 [2048, 5120], P('tile', 'head'), as said below
- query_gain: float32 [5120], P('head'), may hold values from 0.5 to 1.5
- key_gain: float32 [5120], P('head'), may hold values from 0.5 to 1.5
- cross_gain: float32 [5120], P('head'), may hold values from 0.5 to 1.5
- text_gain: float32 [5120], P('head'), may hold values from 0.5 to 1.5
- tile_item: int32 [8], replicated, may hold values from 0 to 3, as said below
- row_count: int32 [8], replicated, may hold values from 32 to 128, as said below
- text_len: int32 [8], replicated, may hold values from 2 to 256, as said below
Outputs:
- attended: bfloat16 [1024, 5120], P('tile', 'head')
The draws below stay inside these ranges and needn't reach their ends.
Inputs may be any that keep to these rules, and one draw needn't show every extreme that they name: `tile_item`: never falling and 0 on the first tile; every item holds 1 to 4 consecutive tiles, some item holds exactly 4, and there are 4 items. `row_count`: some tile holds exactly 128. `text_len`: entries past the last item are not used; some item has exactly 256. `text_key`: tiles of one item hold the same text rows. `text_value`: tiles of one item hold the same text rows.
All inputs are finite; a program needn't handle non-finite values.
Results may differ from the reference program's by a relative error of at most 0.0015.
The reference program's roundings to bfloat16 on the way count: a program that leaves them out, or rounds other values in their place, can miss the bound.
Values may be sent and summed in bfloat16 or wider, within the bound.
A program may use at most 64 MiB of HBM per device.

```python
import math
import jax
import jax.numpy as jnp
from jax import lax

D = 5120
HEADS = 40
HD = 128
ROWS = 128
TXT = 256
HGT = 30
WID = 52
SPAN = 4
TILES = 8
TOKENS = 1024


def layout(key):
    groups = TILES // 2
    pool = (groups - 1) * (SPAN - 1)
    extra = TILES - SPAN - (groups - 1)
    order = jax.random.permutation(jax.random.fold_in(key, 11), pool)
    marked = (order < extra).astype(jnp.int32).reshape(groups - 1, SPAN - 1)
    rest = (1 + jnp.sum(marked, axis=1)).astype(jnp.int32)
    chosen = jax.random.randint(jax.random.fold_in(key, 16), (), 0, groups)
    group_ids = jnp.arange(groups)
    pick = jnp.clip(jnp.where(group_ids < chosen, group_ids, group_ids - 1), 0, groups - 2)
    spans = jnp.where(group_ids == chosen, SPAN, rest[pick]).astype(jnp.int32)
    ends = jnp.cumsum(spans)
    tile_ids = jnp.arange(TILES)
    owner = jnp.sum((ends[None, :] <= tile_ids[:, None]).astype(jnp.int32), axis=1)
    return owner.astype(jnp.int32)


def draw_self_query(key, part):
    base = jax.random.normal(jax.random.fold_in(key, 31), (TOKENS, D), jnp.float32)
    return base.astype(jnp.bfloat16)


def draw_self_key(key, part):
    base = jax.random.normal(jax.random.fold_in(key, 41), (TOKENS, D), jnp.float32)
    return base.astype(jnp.bfloat16)


def draw_cross_query(key, part):
    base = jax.random.normal(jax.random.fold_in(key, 51), (TOKENS, D), jnp.float32)
    return base.astype(jnp.bfloat16)


def draw_text_key(key, part):
    owner = layout(key)
    base = jax.random.normal(jax.random.fold_in(key, 61), (TILES * TXT, D), jnp.float32)
    return base.reshape(TILES, TXT, D)[owner].reshape(TILES * TXT, D).astype(jnp.bfloat16)


def draw_text_value(key, part):
    owner = layout(key)
    base = jax.random.normal(jax.random.fold_in(key, 71), (TILES, TXT, D), jnp.float32)
    return base[owner].reshape(TILES * TXT, D).astype(jnp.bfloat16)


def draw_tile_item(key, part):
    return layout(key)


def draw_row_count(key, part):
    counts = jax.random.randint(jax.random.fold_in(key, 14), (TILES,), ROWS // 4, ROWS + 1)
    chosen = jax.random.randint(jax.random.fold_in(key, 15), (), 0, TILES)
    return jnp.where(jnp.arange(TILES) == chosen, ROWS, counts).astype(jnp.int32)


def draw_text_len(key, part):
    owner = layout(key)
    items = owner[TILES - 1] + 1
    lengths = jax.random.randint(jax.random.fold_in(key, 12), (TILES,), 2, TXT + 1)
    chosen = jax.random.randint(jax.random.fold_in(key, 13), (), 0, items)
    return jnp.where(jnp.arange(TILES) == chosen, TXT, lengths).astype(jnp.int32)


def steps_of(key, shape, shards, least, largest):
    def one(dim, blocks):
        heights = jax.random.uniform(jax.random.fold_in(jax.random.fold_in(key, 6), dim), (blocks,), jnp.float32, least / len(shards), largest / len(shards))
        return jnp.repeat(jnp.exp(heights), shape[dim] // blocks).reshape((-1,) + (1,) * (len(shape) - dim - 1))

    level = one(*shards[0])
    for cut in shards[1:]:
        level = level * one(*cut)
    return level


def bell_draw(own_key, dims, width, bound, shards=(), kind=jnp.bfloat16):
    array = jax.random.normal(own_key, dims, jnp.float32) * width
    if len(shards) > 0:
        array = steps_of(own_key, dims, shards, -0.22, 0.18) * array
    return jnp.clip(array, min=-bound, max=bound).astype(kind)


def setup_inputs(seed: int = 0) -> dict:
    seeds = jax.random.split(jax.random.key(seed), 14)
    self_query = draw_self_query(jax.random.fold_in(seeds[13], 71), 0)
    self_key = draw_self_key(jax.random.fold_in(seeds[13], 71), 0)
    self_value = bell_draw(seeds[2], (TOKENS, D), 1.0, 6.0, ((0, 8), (1, 4)))
    cross_query = draw_cross_query(jax.random.fold_in(seeds[13], 71), 0)
    text_key = draw_text_key(jax.random.fold_in(seeds[13], 71), 0)
    text_value = draw_text_value(jax.random.fold_in(seeds[13], 71), 0)
    query_gain = jnp.clip(1.0 + 0.1 * jax.random.normal(seeds[6], (D,), jnp.float32), 0.5, 1.5)
    key_gain = jnp.clip(1.0 + 0.1 * jax.random.normal(seeds[7], (D,), jnp.float32), 0.5, 1.5)
    cross_gain = jnp.clip(1.0 + 0.1 * jax.random.normal(seeds[8], (D,), jnp.float32), 0.5, 1.5)
    text_gain = jnp.clip(1.0 + 0.1 * jax.random.normal(seeds[9], (D,), jnp.float32), 0.5, 1.5)
    tile_item = draw_tile_item(jax.random.fold_in(seeds[13], 71), 0)
    row_count = draw_row_count(jax.random.fold_in(seeds[13], 71), 0)
    text_len = draw_text_len(jax.random.fold_in(seeds[13], 71), 0)
    return {"self_query": self_query, "self_key": self_key, "self_value": self_value, "cross_query": cross_query, "text_key": text_key, "text_value": text_value, "query_gain": query_gain, "key_gain": key_gain, "cross_gain": cross_gain, "text_gain": text_gain, "tile_item": tile_item, "row_count": row_count, "text_len": text_len}


EPSILON = 1e-06

def frequencies(amount, dimension):
    return 1.0 / 10000.0 ** (jnp.arange(amount, dtype=jnp.float32) * 2.0 / dimension)

def rope_angles(positions):
    spatial = HD // 6
    temporal = HD // 2 - 2 * spatial
    frame = (positions // (HGT * WID)).astype(jnp.float32)
    height = (positions // WID % HGT).astype(jnp.float32)
    across = (positions % WID).astype(jnp.float32)
    return jnp.concatenate([frame[:, None] * frequencies(temporal, 2 * temporal)[None, :], height[:, None] * frequencies(spatial, 2 * spatial)[None, :], across[:, None] * frequencies(spatial, 2 * spatial)[None, :]], axis=1)

def pair_partner(matrix):
    index = jnp.arange(matrix.shape[-1])
    return jnp.where(index % 2 == 0, -jnp.roll(matrix, -1, axis=-1), jnp.roll(matrix, 1, axis=-1))

def rotate(matrix, angle):
    cosine = jnp.repeat(jnp.cos(angle), 2, axis=1)
    sine = jnp.repeat(jnp.sin(angle), 2, axis=1)
    shaped = matrix.reshape(matrix.shape[0], matrix.shape[1] // HD, HD)
    turned = shaped * cosine[:, None, :] + pair_partner(shaped) * sine[:, None, :]
    return turned.reshape(matrix.shape)

def normalize(matrix, gain):
    values = matrix.astype(jnp.float32)
    mean_square = lax.optimization_barrier(jnp.sum(values * values, axis=1)) / D
    return values * lax.rsqrt(mean_square[:, None] + EPSILON) * gain.astype(jnp.float32)[None, :]

def attend(query, key_rows, value_rows, live):
    scale = 1.0 / math.sqrt(HD)
    query_heads = query.astype(jnp.float32).reshape(query.shape[0], HEADS, HD)
    key_heads = key_rows.astype(jnp.float32).reshape(key_rows.shape[0], HEADS, HD)
    value_heads = value_rows.astype(jnp.float32).reshape(value_rows.shape[0], HEADS, HD)
    scores = jnp.einsum('qhd,khd->hqk', query_heads, key_heads) * scale
    scores = jnp.where(live[None, None, :], scores, -1e+30)
    highest = lax.optimization_barrier(jnp.max(scores, axis=2, keepdims=True))
    weights = jnp.exp(scores - highest)
    total = lax.optimization_barrier(jnp.sum(weights, axis=2, keepdims=True))
    rounded = lax.optimization_barrier(weights.astype(jnp.bfloat16)).astype(jnp.float32)
    mixed = jnp.einsum('hqk,khd->qhd', rounded, value_heads) / jnp.moveaxis(total, 0, 1)
    return mixed.reshape(query.shape[0], HEADS * HD)

def reference(self_query, self_key, self_value, cross_query, text_key, text_value, query_gain, key_gain, cross_gain, text_gain, tile_item, row_count, text_len):
    tile_ids = jnp.arange(TILES, dtype=jnp.int32)
    first_tile = lax.optimization_barrier(jnp.sum((tile_item[None, :] < tile_item[:, None]).astype(jnp.int32), axis=1))
    positions = ((tile_ids - first_tile)[:, None] * ROWS + jnp.arange(ROWS, dtype=jnp.int32)[None, :]).reshape(TOKENS)
    angle = rope_angles(positions)
    queries = rotate(normalize(self_query, query_gain), angle).astype(jnp.bfloat16)
    keys = rotate(normalize(self_key, key_gain), angle).astype(jnp.bfloat16)
    cross = normalize(cross_query, cross_gain).astype(jnp.bfloat16)
    texts = normalize(text_key, text_gain).astype(jnp.bfloat16)
    reach = SPAN - 1
    window = 2 * SPAN - 1
    keys_padded = jnp.pad(keys, ((reach * ROWS, reach * ROWS), (0, 0)))
    values_padded = jnp.pad(self_value, ((reach * ROWS, reach * ROWS), (0, 0)))
    items_padded = jnp.pad(tile_item, (reach, reach), constant_values=-1)
    counts_padded = jnp.pad(row_count, (reach, reach))

    def one_tile(tile_index):
        start = (tile_index * ROWS).astype(jnp.int32)
        query = lax.dynamic_slice_in_dim(queries, start, ROWS, 0)
        near_keys = lax.dynamic_slice_in_dim(keys_padded, start, window * ROWS, 0)
        near_values = lax.dynamic_slice_in_dim(values_padded, start, window * ROWS, 0)
        near_items = lax.dynamic_slice_in_dim(items_padded, tile_index.astype(jnp.int32), window, 0)
        near_counts = lax.dynamic_slice_in_dim(counts_padded, tile_index.astype(jnp.int32), window, 0)
        item_here = tile_item[tile_index]
        live = ((near_items == item_here)[:, None] & (jnp.arange(ROWS, dtype=jnp.int32)[None, :] < near_counts[:, None])).reshape(window * ROWS)
        self_part = attend(query, near_keys, near_values, live)
        text_start = (tile_index * TXT).astype(jnp.int32)
        cross_rows = lax.dynamic_slice_in_dim(cross, start, ROWS, 0)
        text_rows = lax.dynamic_slice_in_dim(texts, text_start, TXT, 0)
        text_vals = lax.dynamic_slice_in_dim(text_value, text_start, TXT, 0)
        text_live = jnp.arange(TXT, dtype=jnp.int32) < text_len[item_here]
        text_part = attend(cross_rows, text_rows, text_vals, text_live)
        return (self_part + text_part).astype(jnp.bfloat16)
    return lax.map(one_tile, tile_ids).reshape(TOKENS, D)
```

```python
import functools
import math

import jax
import jax.numpy as jnp
import numpy as np
from jax import lax
from jax.experimental import pallas as pl
from jax.experimental.pallas import tpu as pltpu
from jax.sharding import PartitionSpec as P

D = 5120
HD = 128
HGT = 30
WID = 52


EPSILON = 1e-06


def shifted(value, axis, by):
    peers = lax.axis_size(axis)
    pairs = [(i, i + by) for i in range(peers) if 0 <= i + by < peers]
    return lax.ppermute(value, axis, pairs)


def frequencies(amount, dimension):
    return 1.0 / 10000.0 ** (jnp.arange(amount, dtype=jnp.float32) * 2.0 / dimension)


def rope_angles(positions):
    spatial = HD // 6
    temporal = HD // 2 - 2 * spatial
    frame = (positions // (HGT * WID)).astype(jnp.float32)
    height = (positions // WID % HGT).astype(jnp.float32)
    across = (positions % WID).astype(jnp.float32)
    return jnp.concatenate(
        [
            frame[:, None] * frequencies(temporal, 2 * temporal)[None, :],
            height[:, None] * frequencies(spatial, 2 * spatial)[None, :],
            across[:, None] * frequencies(spatial, 2 * spatial)[None, :],
        ],
        axis=1,
    )


def pair_partner(matrix):
    index = jnp.arange(matrix.shape[-1])
    return jnp.where(index % 2 == 0, -jnp.roll(matrix, -1, axis=-1), jnp.roll(matrix, 1, axis=-1))


def rotate(matrix, angle):
    cosine = jnp.repeat(jnp.cos(angle), 2, axis=1)
    sine = jnp.repeat(jnp.sin(angle), 2, axis=1)
    shaped = matrix.reshape(matrix.shape[0], matrix.shape[1] // HD, HD)
    turned = shaped * cosine[:, None, :] + pair_partner(shaped) * sine[:, None, :]
    return turned.reshape(matrix.shape)


def scaled_rows(values, mean_square, gain):
    return values * lax.rsqrt(mean_square[:, None] + EPSILON) * gain[None, :]


def attend_head(query, key_rows, value_rows, live):
    scale = 1.0 / math.sqrt(HD)
    scores = (
        lax.dot_general(
            query, key_rows, (((1,), (1,)), ((), ())), preferred_element_type=jnp.float32
        )
        * scale
    )
    scores = jnp.where(live[None, :], scores, -1e30)
    highest = jnp.max(scores, axis=1, keepdims=True)
    weights = jnp.exp(scores - highest)
    total = jnp.sum(weights, axis=1, keepdims=True)
    mixed = jnp.dot(weights.astype(jnp.bfloat16), value_rows, preferred_element_type=jnp.float32)
    return mixed / total


def per_device(
    self_query,
    self_key,
    self_value,
    cross_query,
    text_key,
    text_value,
    query_gain,
    key_gain,
    cross_gain,
    text_gain,
    tile_item,
    row_count,
    text_len,
):
    row_total = self_query.shape[0]
    text_total = text_key.shape[0]
    head_total = self_query.shape[1] // HD
    tile_here = lax.axis_index("tile")
    tile_total = lax.axis_size("tile")
    span = min(7, tile_total // 2)
    item_here = tile_item[tile_here]
    first_tile = jnp.sum((tile_item < item_here).astype(jnp.int32))
    positions = (tile_here - first_tile) * row_total + jnp.arange(row_total, dtype=jnp.int32)
    angle = rope_angles(positions)
    query_float = self_query.astype(jnp.float32)
    key_float = self_key.astype(jnp.float32)
    cross_float = cross_query.astype(jnp.float32)
    text_float = text_key.astype(jnp.float32)
    query_sq, key_sq, cross_sq, text_sq = lax.psum(
        (
            jnp.sum(query_float * query_float, axis=1),
            jnp.sum(key_float * key_float, axis=1),
            jnp.sum(cross_float * cross_float, axis=1),
            jnp.sum(text_float * text_float, axis=1),
        ),
        "head",
    )
    queries = rotate(scaled_rows(query_float, query_sq / D, query_gain), angle).astype(jnp.bfloat16)
    rotated_keys = rotate(scaled_rows(key_float, key_sq / D, key_gain), angle).astype(jnp.bfloat16)
    cross = scaled_rows(cross_float, cross_sq / D, cross_gain).astype(jnp.bfloat16)
    texts = scaled_rows(text_float, text_sq / D, text_gain).astype(jnp.bfloat16)

    def live_rows(source):
        inside = (source >= 0) & (source < tile_total)
        clipped = jnp.clip(source, 0, tile_total - 1)
        same_item = inside & (tile_item[clipped] == item_here)
        return same_item & (jnp.arange(row_total, dtype=jnp.int32) < row_count[clipped])

    key_parts = [rotated_keys]
    value_parts = [self_value]
    live_parts = [live_rows(tile_here)]
    for distance in range(1, span):
        for offset in (distance, -distance):
            moved_keys, moved_values = shifted((rotated_keys, self_value), "tile", offset)
            key_parts.append(moved_keys)
            value_parts.append(moved_values)
            live_parts.append(live_rows(tile_here - offset))
    keys_all = jnp.concatenate(key_parts, axis=0)
    values_all = jnp.concatenate(value_parts, axis=0)
    live_all = jnp.concatenate(live_parts, axis=0)
    text_live = jnp.arange(text_total, dtype=jnp.int32) < text_len[item_here]

    def per_head(head_index):
        first_column = head_index * HD

        def columns(matrix):
            return lax.dynamic_slice_in_dim(matrix, first_column, HD, 1)

        local_part = attend_head(columns(queries), columns(keys_all), columns(values_all), live_all)
        text_part = attend_head(columns(cross), columns(texts), columns(text_value), text_live)
        return (local_part + text_part).astype(jnp.bfloat16)

    head_outputs = lax.map(per_head, jnp.arange(head_total, dtype=jnp.int32))
    return jnp.moveaxis(head_outputs, 0, 1).reshape(row_total, head_total * HD)


TILES = 8
SHARDS = 4
SPAN = 4
WIDE = 256
BIG = -1e30


def needs(start):
    found = []
    for t in range(TILES):
        if start <= t < start + SPAN:
            found.append({b for b in range(start, start + SPAN) if b != t})
        else:
            near = {t - 1, t + 1} & set(range(TILES))
            found.append({b for b in near if not start <= b < start + SPAN})
    return found


def window(start):
    return [start if start <= t < start + SPAN else (0 if t < start else TILES - SPAN) for t in range(TILES)]


def chip_edges(start, block, chips, cut):
    home = block // 2
    return [(home, chip) for chip in sorted(chips)]


def edges_of(start, cut):
    need = needs(start)
    edges = []
    for b in range(TILES):
        users = [t for t in range(TILES) if b in need[t]]
        home, core = b // 2, b % 2
        held = {home: (b, 0)}
        if b ^ 1 in users:
            edges.append((b, b ^ 1, b, 0))
        chips = {t // 2 for t in users} - {home}
        for a, c in chip_edges(start, b, chips, cut):
            src, depth = held[a]
            same = 2 * c + core
            onward = any(x == c for x, _ in chip_edges(start, b, chips, cut))
            entry = same if same in users or onward or same ^ 1 not in users else same ^ 1
            edges.append((src, entry, b, depth))
            held[c] = (entry, depth + 1)
            if entry ^ 1 in users:
                edges.append((entry, entry ^ 1, b, depth + 1))
    return edges


def plan_of(start, cut):
    edges = edges_of(start, cut)
    first = [[e[1] for e in sorted(edges) if e[3] == 0 and e[0] == t] for t in range(TILES)]
    first = [sorted(f, key=lambda v, t=t: v == t ^ 1) for t, f in enumerate(first)]
    rounds = []
    for depth in range(1, 1 + max([e[3] for e in edges])):
        events = []
        for t in range(TILES):
            mine = sorted({e[2] for e in edges if e[3] == depth and e[0] == t})
            dests = [(b, sorted([e[1] for e in edges if e[0] == t and e[2] == b], key=lambda v: v == t ^ 1)) for b in mine]
            events.append(dests)
        for k in range(max(len(e) for e in events)):
            rounds.append([e[k] if k < len(e) else None for e in events])
    gets = [{e[2] for e in edges if e[1] == t} for t in range(TILES)]
    passed = [{e[2] for e in edges if e[3] > 0 and e[0] == t} for t in range(TILES)]
    return first, rounds, gets, passed


def kernel(
    start,
    q_in, k_in, v_in, c_in, tk_in, tv_in,
    q_gain, k_gain, c_gain, t_gain,
    cos_ref, sin_ref, tile_item, row_count, text_len,
    out_ref,
    q_raw, k_raw, c_raw, t_raw, t_val,
    queries, cross, texts, text_out,
    kbuf, vbuf, sums, live, text_live,
    in_sem, z_send, z_recv, send_sem, recv_sem,
):
    me = lax.axis_index("tile")
    shard = lax.axis_index("head")
    rows = q_in.shape[0]
    heads = q_in.shape[1] // HD
    groups = q_in.shape[1] // WIDE
    per = WIDE // HD
    txt = tk_in.shape[0]

    def pick(values):
        result = jnp.int32(values[0])
        for i in range(1, TILES):
            if values[i] != values[0]:
                result = jnp.where(me == i, jnp.int32(values[i]), result)
        return result

    loads = [
        pltpu.make_async_copy(src, dst, in_sem.at[i])
        for i, (src, dst) in enumerate(
            ((k_in, k_raw), (q_in, q_raw), (c_in, c_raw), (tk_in, t_raw), (tv_in, t_val))
        )
    ]
    own = [
        pltpu.make_async_copy(v_in.at[:, g * WIDE : (g + 1) * WIDE], vbuf.at[me, g], in_sem.at[5 + g])
        for g in range(groups)
    ]
    for load in loads + own:
        load.start()

    barrier = pltpu.get_barrier_semaphore()
    for o in range(1, TILES):
        pl.semaphore_signal(barrier, inc=1, device_id=(lax.rem(me + o, TILES), shard), device_id_type=pl.DeviceIdType.MESH)
    for o in range(1, SHARDS):
        pl.semaphore_signal(barrier, inc=1, device_id=(me, lax.rem(shard + o, SHARDS)), device_id_type=pl.DeviceIdType.MESH)
    pl.semaphore_wait(barrier, TILES + SHARDS - 2)

    plan = plan_of(start, 0)
    first, rounds, gets, passed = plan
    fan = max(len(f) for f in first)
    base = pick(window(start))

    def send(src, buf, kind, block, g, lane, dest):
        return pltpu.make_async_remote_copy(
            src_ref=src,
            dst_ref=buf.at[block, g],
            send_sem=send_sem.at[kind, block, g, lane],
            recv_sem=recv_sem.at[kind, block, g],
            device_id=(dest, shard),
            device_id_type=pl.DeviceIdType.MESH,
        )

    def each_first(act):
        for lane in range(fan):
            dests = [f[lane] if lane < len(f) else -1 for f in first]
            dest = pick(dests)

            def run(lane=lane, dest=dest):
                act(lane, dest)

            if -1 in dests:
                pl.when(dest >= 0)(run)
            else:
                run()

    def each_round(act):
        for one in rounds:
            block = pick([e[0] if e else -1 for e in one])
            widest = max(len(e[1]) for e in one if e)
            dests = [pick([e[1][i] if e and i < len(e[1]) else -1 for e in one]) for i in range(widest)]

            def run(block=block, dests=dests):
                act(block, dests)

            if any(e is None for e in one):
                pl.when(block >= 0)(run)
            else:
                run()

    def pass_on(buf, kind, g):
        def act(block, dests):
            send(buf.at[block, g], buf, kind, block, g, 0, me).wait_recv()
            for lane, dest in enumerate(dests):

                def go(lane=lane, dest=dest):
                    send(buf.at[block, g], buf, kind, block, g, lane, dest).start()

                pl.when(dest >= 0)(go)

        each_round(act)

    def arrive(buf, kind, g):
        for j in range(SPAN):
            waits = [int(window(start)[t] + j in gets[t] and window(start)[t] + j not in passed[t]) for t in range(TILES)]

            def go(j=j):
                send(buf.at[base + j, g], buf, kind, base + j, g, 0, me).wait_recv()

            if any(waits):
                pl.when(pick(waits) == 1)(go)

    def drain(buf, kind, g):
        def of_first(lane, dest):
            send(buf.at[me, g], buf, kind, me, g, lane, dest).wait_send()

        each_first(of_first)

        def of_round(block, dests):
            for lane, dest in enumerate(dests):

                def go(lane=lane, dest=dest):
                    send(buf.at[block, g], buf, kind, block, g, lane, dest).wait_send()

                pl.when(dest >= 0)(go)

        each_round(of_round)

    for g in range(groups):
        own[g].wait()

        def of_value(lane, dest, g=g):
            send(vbuf.at[me, g], vbuf, 0, me, g, lane, dest).start()

        each_first(of_value)

    for j in range(SPAN):
        empty = [int(window(start)[t] + j not in gets[t] and window(start)[t] + j != t) for t in range(TILES)]
        if any(empty):

            @pl.when(pick(empty) == 1)
            def _(j=j):
                vbuf[base + j] = jnp.zeros((groups, rows, WIDE), jnp.bfloat16)

    def partial(ref, r0):
        total = jnp.zeros((rows, HD), jnp.float32)
        for i in range(heads):
            part = ref[r0 : r0 + rows, i * HD : (i + 1) * HD].astype(jnp.float32)
            total = total + part * part
        column = jnp.sum(total, axis=1, keepdims=True)
        return jnp.broadcast_to(column, (rows, HD)).T[0:8, :]

    for load in loads[:4]:
        load.wait()
    pieces = [(k_raw, 0), (q_raw, 0), (c_raw, 0)] + [(t_raw, r) for r in range(0, txt, rows)]
    for i, (ref, r0) in enumerate(pieces):
        sums[shard, :, i * rows : (i + 1) * rows] = partial(ref, r0)

    def share(o, slot):
        return pltpu.make_async_remote_copy(
            src_ref=sums.at[slot],
            dst_ref=sums.at[slot],
            send_sem=z_send.at[o - 1],
            recv_sem=z_recv.at[slot],
            device_id=(me, lax.rem(shard + o, SHARDS)),
            device_id_type=pl.DeviceIdType.MESH,
        )

    for o in range(1, SHARDS):
        share(o, shard).start()

    item = tile_item[me]
    before = jnp.int32(0)
    for t in range(TILES):
        before = before + jnp.where(tile_item[t] < item, 1, 0).astype(jnp.int32)
    place = me - before
    words = jnp.int32(0)
    for t in range(TILES):
        words = words + jnp.where(item == t, text_len[t], 0).astype(jnp.int32)
    lane_row = lax.broadcasted_iota(jnp.int32, (8, rows), 1)
    for j in range(SPAN):
        block = base + j
        limit = jnp.where(tile_item[block] == item, row_count[block], 0)
        live[:, j * rows : (j + 1) * rows] = jnp.where(lane_row < limit, 0.0, 1.0).astype(jnp.float32)
    lane_text = lax.broadcasted_iota(jnp.int32, (8, txt), 1)
    text_live[...] = jnp.where(lane_text < words, 0.0, 1.0).astype(jnp.float32)

    for o in range(1, SHARDS):
        share(o, lax.rem(shard + o, SHARDS)).wait_recv()

    def scale_of(i):
        span = slice(i * rows, (i + 1) * rows)
        total = (sums[0, :, span] + sums[1, :, span]) + (sums[2, :, span] + sums[3, :, span])
        scale = lax.rsqrt(total / D + EPSILON)
        return jnp.broadcast_to(scale[0:1, :], (HD, rows)).T

    cosine = cos_ref[0:rows, :]
    sine = sin_ref[0:rows, :]
    for j in range(1, SPAN):
        cosine = jnp.where(place == j, cos_ref[j * rows : (j + 1) * rows, :], cosine)
        sine = jnp.where(place == j, sin_ref[j * rows : (j + 1) * rows, :], sine)
    even = lax.broadcasted_iota(jnp.int32, (rows, HD), 1) % 2 == 0

    def turned(values):
        partner = jnp.where(even, pltpu.roll(values, HD - 1, 1), pltpu.roll(values, 1, 1))
        return values * cosine + partner * sine

    k_scale = scale_of(0)
    for g in range(groups):
        for i in range(per):
            cols = slice(g * WIDE + i * HD, g * WIDE + (i + 1) * HD)
            scaled = k_raw[:, cols].astype(jnp.float32) * k_scale * k_gain[:, cols]
            kbuf[me, g, :, i * HD : (i + 1) * HD] = turned(scaled).astype(jnp.bfloat16)

        def of_key(lane, dest, g=g):
            send(kbuf.at[me, g], kbuf, 1, me, g, lane, dest).start()

        each_first(of_key)

    q_scale = scale_of(1)
    for i in range(heads):
        cols = slice(i * HD, (i + 1) * HD)
        scaled = q_raw[:, cols].astype(jnp.float32) * q_scale * q_gain[:, cols]
        queries[i // per, :, (i % per) * HD : (i % per + 1) * HD] = turned(scaled).astype(jnp.bfloat16)
    c_scale = scale_of(2)
    for i in range(heads):
        cols = slice(i * HD, (i + 1) * HD)
        cross[i // per, :, (i % per) * HD : (i % per + 1) * HD] = (
            c_raw[:, cols].astype(jnp.float32) * c_scale * c_gain[:, cols]
        ).astype(jnp.bfloat16)
    for r in range(txt // rows):
        t_scale = scale_of(3 + r)
        span = slice(r * rows, (r + 1) * rows)
        for i in range(heads):
            cols = slice(i * HD, (i + 1) * HD)
            texts[i // per, span, (i % per) * HD : (i % per + 1) * HD] = (
                t_raw[span, cols].astype(jnp.float32) * t_scale * t_gain[:, cols]
            ).astype(jnp.bfloat16)

    scale = 1.0 / math.sqrt(HD)

    def weigh(scores, dead):
        scores = jnp.where(dead > 0.5, BIG, scores * scale)
        highest = jnp.max(scores, axis=1, keepdims=True)
        weights = jnp.exp(scores - highest)
        total = jnp.sum(weights, axis=1, keepdims=True)
        return weights.astype(jnp.bfloat16), total

    def against(query, key):
        return lax.dot_general(query, key, (((1,), (1,)), ((), ())), preferred_element_type=jnp.float32)

    loads[4].wait()

    def text_group(g, carry):
        dead = text_live[0:1, :]
        for i in range(per):
            cols = slice(i * HD, (i + 1) * HD)
            at = pl.ds(pl.multiple_of(g * WIDE + i * HD, HD), HD)
            weights, total = weigh(against(cross[g, :, cols], texts[g, :, cols]), dead)
            mixed = jnp.dot(weights, t_val[:, at], preferred_element_type=jnp.float32)
            text_out[g, :, cols] = mixed / total
        pass_on(vbuf, 0, g)
        return carry

    lax.fori_loop(0, groups, text_group, 0)

    def self_group(g, carry):
        pass_on(kbuf, 1, g)
        arrive(vbuf, 0, g)
        arrive(kbuf, 1, g)
        dead = live[0:1, :]
        for i in range(per):
            cols = slice(i * HD, (i + 1) * HD)
            query = queries[g, :, cols]
            scores = jnp.concatenate([against(query, kbuf[base + j, g, :, cols]) for j in range(SPAN)], axis=1)
            weights, total = weigh(scores, dead)
            mixed = jnp.zeros((rows, HD), jnp.float32)
            for j in range(SPAN):
                mixed = mixed + jnp.dot(
                    weights[:, j * rows : (j + 1) * rows], vbuf[base + j, g, :, cols], preferred_element_type=jnp.float32
                )
            at = pl.ds(pl.multiple_of(g * WIDE + i * HD, HD), HD)
            out_ref[:, at] = (mixed / total + text_out[g, :, cols]).astype(jnp.bfloat16)
        return carry

    lax.fori_loop(0, groups, self_group, 0)

    def finish(g, carry):
        drain(vbuf, 0, g)
        drain(kbuf, 1, g)
        return carry

    lax.fori_loop(0, groups, finish, 0)
    for o in range(1, SHARDS):
        share(o, shard).wait_send()


def rotary_tables(rows):
    positions = np.arange(SPAN * rows)
    spatial = HD // 6
    temporal = HD // 2 - 2 * spatial

    def rates(amount):
        return (1.0 / 10000.0 ** (np.arange(amount) / amount)).astype(np.float32)

    angle = np.concatenate(
        [
            (positions // (HGT * WID)).astype(np.float32)[:, None] * rates(temporal)[None, :],
            (positions // WID % HGT).astype(np.float32)[:, None] * rates(spatial)[None, :],
            (positions % WID).astype(np.float32)[:, None] * rates(spatial)[None, :],
        ],
        axis=1,
    ).astype(np.float64)
    cosine = np.repeat(np.cos(angle), 2, axis=1).astype(np.float32)
    sine = np.repeat(np.sin(angle), 2, axis=1).astype(np.float32)
    sine[:, 0::2] *= -1.0
    return cosine, sine


def fused(
    self_query, self_key, self_value, cross_query, text_key, text_value,
    query_gain, key_gain, cross_gain, text_gain, tile_item, row_count, text_len,
):
    rows, width = self_query.shape
    txt = text_key.shape[0]
    groups = width // WIDE
    cosine, sine = rotary_tables(rows)
    bf16, f32 = jnp.bfloat16, jnp.float32
    hbm = pl.BlockSpec(memory_space=pl.ANY)
    vmem = pl.BlockSpec(memory_space=pltpu.VMEM)
    smem = pl.BlockSpec(memory_space=pltpu.SMEM)

    def call(start):
        return pl.pallas_call(
            functools.partial(kernel, start),
            out_shape=jax.ShapeDtypeStruct((rows, width), bf16),
            in_specs=[hbm] * 6 + [vmem] * 6 + [smem] * 3,
            out_specs=vmem,
            scratch_shapes=[
                pltpu.VMEM((rows, width), bf16),
                pltpu.VMEM((rows, width), bf16),
                pltpu.VMEM((rows, width), bf16),
                pltpu.VMEM((txt, width), bf16),
                pltpu.VMEM((txt, width), bf16),
                pltpu.VMEM((groups, rows, WIDE), bf16),
                pltpu.VMEM((groups, rows, WIDE), bf16),
                pltpu.VMEM((groups, txt, WIDE), bf16),
                pltpu.VMEM((groups, rows, WIDE), f32),
                pltpu.VMEM((TILES, groups, rows, WIDE), bf16),
                pltpu.VMEM((TILES, groups, rows, WIDE), bf16),
                pltpu.VMEM((SHARDS, 8, 3 * rows + txt), f32),
                pltpu.VMEM((8, SPAN * rows), f32),
                pltpu.VMEM((8, txt), f32),
                pltpu.SemaphoreType.DMA((5 + groups,)),
                pltpu.SemaphoreType.DMA((SHARDS - 1,)),
                pltpu.SemaphoreType.DMA((SHARDS,)),
                pltpu.SemaphoreType.DMA((2, TILES, groups, 4)),
                pltpu.SemaphoreType.DMA((2, TILES, groups)),
            ],
            compiler_params=pltpu.CompilerParams(
                collective_id=start, has_side_effects=True, vmem_limit_bytes=40 * 1024 * 1024
            ),
        )

    operands = (
        self_query, self_key, self_value, cross_query, text_key, text_value,
        query_gain[None, :], key_gain[None, :], cross_gain[None, :], text_gain[None, :],
        jnp.asarray(cosine), jnp.asarray(sine), tile_item, row_count, text_len,
    )
    full = tile_item[SPAN - 1 :] == tile_item[: TILES - SPAN + 1]
    start = jnp.argmax(full).astype(jnp.int32)
    return lax.switch(start, [call(s) for s in range(TILES - SPAN + 1)], *operands)


def solution(mesh):
    in_specs = (
        P("tile", "head"),
        P("tile", "head"),
        P("tile", "head"),
        P("tile", "head"),
        P("tile", "head"),
        P("tile", "head"),
        P("head"),
        P("head"),
        P("head"),
        P("head"),
        P(),
        P(),
        P(),
    )
    out_specs = P("tile", "head")
    small = mesh.shape["tile"] == TILES and mesh.shape["head"] == SHARDS
    return jax.shard_map(
        fused if small else per_device, mesh=mesh, in_specs=in_specs, out_specs=out_specs, check_vma=False
    )
```

```python
import functools
import math

import jax
import jax.numpy as jnp
import numpy as np
from jax import lax
from jax.experimental import pallas as pl
from jax.experimental.pallas import tpu as pltpu
from jax.sharding import PartitionSpec as P

D = 5120
HD = 128
HGT = 30
WID = 52


EPSILON = 1e-06


def shifted(value, axis, by):
    peers = lax.axis_size(axis)
    pairs = [(i, i + by) for i in range(peers) if 0 <= i + by < peers]
    return lax.ppermute(value, axis, pairs)


def frequencies(amount, dimension):
    return 1.0 / 10000.0 ** (jnp.arange(amount, dtype=jnp.float32) * 2.0 / dimension)


def rope_angles(positions):
    spatial = HD // 6
    temporal = HD // 2 - 2 * spatial
    frame = (positions // (HGT * WID)).astype(jnp.float32)
    height = (positions // WID % HGT).astype(jnp.float32)
    across = (positions % WID).astype(jnp.float32)
    return jnp.concatenate(
        [
            frame[:, None] * frequencies(temporal, 2 * temporal)[None, :],
            height[:, None] * frequencies(spatial, 2 * spatial)[None, :],
            across[:, None] * frequencies(spatial, 2 * spatial)[None, :],
        ],
        axis=1,
    )


def pair_partner(matrix):
    index = jnp.arange(matrix.shape[-1])
    return jnp.where(index % 2 == 0, -jnp.roll(matrix, -1, axis=-1), jnp.roll(matrix, 1, axis=-1))


def rotate(matrix, angle):
    cosine = jnp.repeat(jnp.cos(angle), 2, axis=1)
    sine = jnp.repeat(jnp.sin(angle), 2, axis=1)
    shaped = matrix.reshape(matrix.shape[0], matrix.shape[1] // HD, HD)
    turned = shaped * cosine[:, None, :] + pair_partner(shaped) * sine[:, None, :]
    return turned.reshape(matrix.shape)


def scaled_rows(values, mean_square, gain):
    return values * lax.rsqrt(mean_square[:, None] + EPSILON) * gain[None, :]


def attend_head(query, key_rows, value_rows, live):
    scale = 1.0 / math.sqrt(HD)
    scores = (
        lax.dot_general(
            query, key_rows, (((1,), (1,)), ((), ())), preferred_element_type=jnp.float32
        )
        * scale
    )
    scores = jnp.where(live[None, :], scores, -1e30)
    highest = jnp.max(scores, axis=1, keepdims=True)
    weights = jnp.exp(scores - highest)
    total = jnp.sum(weights, axis=1, keepdims=True)
    mixed = jnp.dot(weights.astype(jnp.bfloat16), value_rows, preferred_element_type=jnp.float32)
    return mixed / total


def per_device(
    self_query,
    self_key,
    self_value,
    cross_query,
    text_key,
    text_value,
    query_gain,
    key_gain,
    cross_gain,
    text_gain,
    tile_item,
    row_count,
    text_len,
):
    row_total = self_query.shape[0]
    text_total = text_key.shape[0]
    head_total = self_query.shape[1] // HD
    tile_here = lax.axis_index("tile")
    tile_total = lax.axis_size("tile")
    span = min(7, tile_total // 2)
    item_here = tile_item[tile_here]
    first_tile = jnp.sum((tile_item < item_here).astype(jnp.int32))
    positions = (tile_here - first_tile) * row_total + jnp.arange(row_total, dtype=jnp.int32)
    angle = rope_angles(positions)
    query_float = self_query.astype(jnp.float32)
    key_float = self_key.astype(jnp.float32)
    cross_float = cross_query.astype(jnp.float32)
    text_float = text_key.astype(jnp.float32)
    query_sq, key_sq, cross_sq, text_sq = lax.psum(
        (
            jnp.sum(query_float * query_float, axis=1),
            jnp.sum(key_float * key_float, axis=1),
            jnp.sum(cross_float * cross_float, axis=1),
            jnp.sum(text_float * text_float, axis=1),
        ),
        "head",
    )
    queries = rotate(scaled_rows(query_float, query_sq / D, query_gain), angle).astype(jnp.bfloat16)
    rotated_keys = rotate(scaled_rows(key_float, key_sq / D, key_gain), angle).astype(jnp.bfloat16)
    cross = scaled_rows(cross_float, cross_sq / D, cross_gain).astype(jnp.bfloat16)
    texts = scaled_rows(text_float, text_sq / D, text_gain).astype(jnp.bfloat16)

    def live_rows(source):
        inside = (source >= 0) & (source < tile_total)
        clipped = jnp.clip(source, 0, tile_total - 1)
        same_item = inside & (tile_item[clipped] == item_here)
        return same_item & (jnp.arange(row_total, dtype=jnp.int32) < row_count[clipped])

    key_parts = [rotated_keys]
    value_parts = [self_value]
    live_parts = [live_rows(tile_here)]
    for distance in range(1, span):
        for offset in (distance, -distance):
            moved_keys, moved_values = shifted((rotated_keys, self_value), "tile", offset)
            key_parts.append(moved_keys)
            value_parts.append(moved_values)
            live_parts.append(live_rows(tile_here - offset))
    keys_all = jnp.concatenate(key_parts, axis=0)
    values_all = jnp.concatenate(value_parts, axis=0)
    live_all = jnp.concatenate(live_parts, axis=0)
    text_live = jnp.arange(text_total, dtype=jnp.int32) < text_len[item_here]

    def per_head(head_index):
        first_column = head_index * HD

        def columns(matrix):
            return lax.dynamic_slice_in_dim(matrix, first_column, HD, 1)

        local_part = attend_head(columns(queries), columns(keys_all), columns(values_all), live_all)
        text_part = attend_head(columns(cross), columns(texts), columns(text_value), text_live)
        return (local_part + text_part).astype(jnp.bfloat16)

    head_outputs = lax.map(per_head, jnp.arange(head_total, dtype=jnp.int32))
    return jnp.moveaxis(head_outputs, 0, 1).reshape(row_total, head_total * HD)


TILES = 8
SHARDS = 4
SPAN = 4
WIDE = 256
BIG = -1e30


def needs(start):
    found = []
    for t in range(TILES):
        if start <= t < start + SPAN:
            found.append({b for b in range(start, start + SPAN) if b != t})
        else:
            near = {t - 1, t + 1} & set(range(TILES))
            found.append({b for b in near if not start <= b < start + SPAN})
    return found


def window(start):
    return [start if start <= t < start + SPAN else (0 if t < start else TILES - SPAN) for t in range(TILES)]


def chip_edges(start, block, chips, far):
    if start > 2:
        return [(3 - a, 3 - c) for a, c in chip_edges(TILES - SPAN - start, TILES - 1 - block, {3 - c for c in chips}, far)]
    home = block // 2
    if start == 0 and block < SPAN and far:
        return [(0, 2), (2, 3), (3, 1)] if home == 0 else [(1, 3), (3, 2), (2, 0)]
    if start == 1 and block in (2, 3, 4):
        return {2: [(1, 0), (0, 2)], 3: [(1, 0), (1, 3), (3, 2)], 4: [(2, 0), (2, 3), (3, 1)]}[block]
    if start == 2 and 2 <= block <= 5:
        return {2: [(1, 0), (0, 2)], 3: [(1, 3), (3, 2)], 4: [(2, 3), (3, 1)], 5: [(2, 0), (0, 1)]}[block]
    return [(home, chip) for chip in sorted(chips)]


def edges_of(start, far):
    need = needs(start)
    edges = []
    for b in range(TILES):
        users = [t for t in range(TILES) if b in need[t]]
        home, core = b // 2, b % 2
        held = {home: (b, 0)}
        if b ^ 1 in users:
            edges.append((b, b ^ 1, b, 0))
        chips = {t // 2 for t in users} - {home}
        for a, c in chip_edges(start, b, chips, far):
            src, depth = held[a]
            same = 2 * c + core
            onward = any(x == c for x, _ in chip_edges(start, b, chips, far))
            entry = same if same in users or onward or same ^ 1 not in users else same ^ 1
            edges.append((src, entry, b, depth))
            held[c] = (entry, depth + 1)
            if entry ^ 1 in users:
                edges.append((entry, entry ^ 1, b, depth + 1))
    return edges


def plan_of(start, far):
    edges = edges_of(start, far)
    first = [[e[1] for e in sorted(edges) if e[3] == 0 and e[0] == t] for t in range(TILES)]
    first = [sorted(f, key=lambda v, t=t: v == t ^ 1) for t, f in enumerate(first)]
    rounds = []
    for depth in range(1, 1 + max([e[3] for e in edges])):
        events = []
        for t in range(TILES):
            mine = sorted({e[2] for e in edges if e[3] == depth and e[0] == t})
            dests = [(b, sorted([e[1] for e in edges if e[0] == t and e[2] == b], key=lambda v: v == t ^ 1)) for b in mine]
            events.append(dests)
        for k in range(max(len(e) for e in events)):
            rounds.append([e[k] if k < len(e) else None for e in events])
    gets = [{e[2] for e in edges if e[1] == t} for t in range(TILES)]
    passed = [{e[2] for e in edges if e[3] > 0 and e[0] == t} for t in range(TILES)]
    return first, rounds, gets, passed


def kernel(
    start,
    q_in, k_in, v_in, c_in, tk_in, tv_in,
    q_gain_in, k_gain_in, c_gain_in, t_gain_in,
    cos_in, sin_in, item_in, count_in, len_in,
    out_ref,
    q_gain, k_gain, c_gain, t_gain,
    cos_ref, sin_ref, tile_item, row_count, text_len,
    q_raw, k_raw, c_raw, t_raw, t_val,
    queries, cross, texts, text_out,
    kbuf, vbuf, sums, live, text_live,
    in_sem, y_send, y_recv, z_send, z_recv, send_sem, recv_sem,
):
    me = lax.axis_index("tile")
    shard = lax.axis_index("head")
    rows = q_in.shape[0]
    heads = q_in.shape[1] // HD
    groups = q_in.shape[1] // WIDE
    per = WIDE // HD
    txt = tk_in.shape[0]

    def pick(values):
        result = jnp.int32(values[0])
        for i in range(1, TILES):
            if values[i] != values[0]:
                result = jnp.where(me == i, jnp.int32(values[i]), result)
        return result

    loads = [
        pltpu.make_async_copy(src, dst, in_sem.at[i])
        for i, (src, dst) in enumerate(
            ((k_in, k_raw), (q_in, q_raw), (c_in, c_raw), (tk_in, t_raw), (tv_in, t_val),
             (item_in, tile_item), (count_in, row_count), (len_in, text_len), (cos_in, cos_ref), (sin_in, sin_ref),
             (k_gain_in, k_gain), (q_gain_in, q_gain), (c_gain_in, c_gain), (t_gain_in, t_gain))
        )
    ]
    own = [
        pltpu.make_async_copy(v_in.at[:, g * WIDE : (g + 1) * WIDE], vbuf.at[me, g], in_sem.at[len(loads) + g])
        for g in range(groups)
    ]
    for load in own + loads:
        load.start()

    barrier = pltpu.get_barrier_semaphore()
    for o in range(1, TILES):
        pl.semaphore_signal(barrier, inc=1, device_id=(lax.rem(me + o, TILES), shard), device_id_type=pl.DeviceIdType.MESH)
    for o in range(1, SHARDS):
        pl.semaphore_signal(barrier, inc=1, device_id=(me, lax.rem(shard + o, SHARDS)), device_id_type=pl.DeviceIdType.MESH)
    pl.semaphore_wait(barrier, TILES + SHARDS - 2)

    near, far = plan_of(start, False), plan_of(start, True)
    split = start in (0, TILES - SPAN)
    order = ([groups - 1] if split else []) + list(range(groups - 1 if split else groups))
    base = pick(window(start))

    def plan(g):
        return far if split and g == groups - 1 else near

    def send(src, buf, kind, block, g, lane, dest):
        return pltpu.make_async_remote_copy(
            src_ref=src,
            dst_ref=buf.at[block, g],
            send_sem=send_sem.at[kind, block, g, lane],
            recv_sem=recv_sem.at[kind, block, g],
            device_id=(dest, shard),
            device_id_type=pl.DeviceIdType.MESH,
        )

    def each_first(first, act):
        for lane in range(max(len(f) for f in first)):
            dests = [f[lane] if lane < len(f) else -1 for f in first]
            dest = pick(dests)

            def run(lane=lane, dest=dest):
                act(lane, dest)

            if -1 in dests:
                pl.when(dest >= 0)(run)
            else:
                run()

    def each_round(rounds, act):
        for one in rounds:
            block = pick([e[0] if e else -1 for e in one])
            widest = max(len(e[1]) for e in one if e)
            dests = [pick([e[1][i] if e and i < len(e[1]) else -1 for e in one]) for i in range(widest)]

            def run(block=block, dests=dests):
                act(block, dests)

            if any(e is None for e in one):
                pl.when(block >= 0)(run)
            else:
                run()

    def pass_on(rounds, buf, kind, g):
        def act(block, dests):
            send(buf.at[block, g], buf, kind, block, g, 0, me).wait_recv()
            for lane, dest in enumerate(dests):

                def go(lane=lane, dest=dest):
                    send(buf.at[block, g], buf, kind, block, g, lane, dest).start()

                pl.when(dest >= 0)(go)

        each_round(rounds, act)

    def arrive(which, buf, kind, g):
        _, _, gets, passed = which
        for j in range(SPAN):
            waits = [int(window(start)[t] + j in gets[t] and window(start)[t] + j not in passed[t]) for t in range(TILES)]

            def go(j=j):
                send(buf.at[base + j, g], buf, kind, base + j, g, 0, me).wait_recv()

            if any(waits):
                pl.when(pick(waits) == 1)(go)

    def drain(which, buf, kind, g):
        def of_first(lane, dest):
            send(buf.at[me, g], buf, kind, me, g, lane, dest).wait_send()

        each_first(which[0], of_first)

        def of_round(block, dests):
            for lane, dest in enumerate(dests):

                def go(lane=lane, dest=dest):
                    send(buf.at[block, g], buf, kind, block, g, lane, dest).wait_send()

                pl.when(dest >= 0)(go)

        each_round(which[1], of_round)

    for g in order:
        own[g].wait()

        def of_value(lane, dest, g=g):
            send(vbuf.at[me, g], vbuf, 0, me, g, lane, dest).start()

        each_first(plan(g)[0], of_value)

    for which, g0, g1 in ((near, 0, groups - 1 if split else groups), (far, groups - 1, groups)):
        if g1 == groups and which is far and not split:
            continue
        for j in range(SPAN):
            empty = [int(window(start)[t] + j not in which[2][t] and window(start)[t] + j != t) for t in range(TILES)]
            if any(empty):

                @pl.when(pick(empty) == 1)
                def _(j=j, g0=g0, g1=g1):
                    for g in range(g0, g1):
                        vbuf[base + j, g] = jnp.zeros((rows, WIDE), jnp.bfloat16)

    def partial(ref, r0):
        total = jnp.zeros((rows, HD), jnp.float32)
        for i in range(heads):
            part = ref[r0 : r0 + rows, i * HD : (i + 1) * HD].astype(jnp.float32)
            total = total + part * part
        column = jnp.sum(total, axis=1, keepdims=True)
        return jnp.broadcast_to(column, (rows, HD)).T[0:8, :]

    def share(o, slot, first):
        span = pl.ds(0, rows) if first else pl.ds(rows, 2 * rows + txt)
        return pltpu.make_async_remote_copy(
            src_ref=sums.at[slot, :, span],
            dst_ref=sums.at[slot, :, span],
            send_sem=(y_send if first else z_send).at[o - 1],
            recv_sem=(y_recv if first else z_recv).at[slot],
            device_id=(me, lax.rem(shard + o, SHARDS)),
            device_id_type=pl.DeviceIdType.MESH,
        )

    def gather(first):
        for o in range(1, SHARDS):
            share(o, lax.rem(shard + o, SHARDS), first).wait_recv()

    pieces = [(k_raw, 0), (q_raw, 0), (c_raw, 0)] + [(t_raw, r) for r in range(0, txt, rows)]
    for i, (ref, r0) in enumerate(pieces):
        if i < 4:
            loads[i].wait()
        sums[shard, :, i * rows : (i + 1) * rows] = partial(ref, r0)
        if i in (0, len(pieces) - 1):
            for o in range(1, SHARDS):
                share(o, shard, i == 0).start()

    for load in loads[5:]:
        load.wait()
    item = tile_item[me]
    before = jnp.int32(0)
    for t in range(TILES):
        before = before + jnp.where(tile_item[t] < item, 1, 0).astype(jnp.int32)
    place = me - before
    words = jnp.int32(0)
    for t in range(TILES):
        words = words + jnp.where(item == t, text_len[t], 0).astype(jnp.int32)
    lane_row = lax.broadcasted_iota(jnp.int32, (8, rows), 1)
    for j in range(SPAN):
        block = base + j
        limit = jnp.where(tile_item[block] == item, row_count[block], 0)
        live[:, j * rows : (j + 1) * rows] = jnp.where(lane_row < limit, 0.0, 1.0).astype(jnp.float32)
    lane_text = lax.broadcasted_iota(jnp.int32, (8, txt), 1)
    text_live[...] = jnp.where(lane_text < words, 0.0, 1.0).astype(jnp.float32)

    gather(True)

    def scale_of(i):
        span = slice(i * rows, (i + 1) * rows)
        total = (sums[0, :, span] + sums[1, :, span]) + (sums[2, :, span] + sums[3, :, span])
        scale = lax.rsqrt(total / D + EPSILON)
        return jnp.broadcast_to(scale[0:1, :], (HD, rows)).T

    cosine = cos_ref[0:rows, :]
    sine = sin_ref[0:rows, :]
    for j in range(1, SPAN):
        cosine = jnp.where(place == j, cos_ref[j * rows : (j + 1) * rows, :], cosine)
        sine = jnp.where(place == j, sin_ref[j * rows : (j + 1) * rows, :], sine)
    even = lax.broadcasted_iota(jnp.int32, (rows, HD), 1) % 2 == 0

    def turned(values):
        partner = jnp.where(even, pltpu.roll(values, HD - 1, 1), pltpu.roll(values, 1, 1))
        return values * cosine + partner * sine

    k_scale = scale_of(0)
    for g in order:
        for i in range(per):
            cols = slice(g * WIDE + i * HD, g * WIDE + (i + 1) * HD)
            scaled = k_raw[:, cols].astype(jnp.float32) * k_scale * k_gain[cols][None, :]
            kbuf[me, g, :, i * HD : (i + 1) * HD] = turned(scaled).astype(jnp.bfloat16)

        def of_key(lane, dest, g=g):
            send(kbuf.at[me, g], kbuf, 1, me, g, lane, dest).start()

        each_first(plan(g)[0], of_key)

    due = [(groups - 1, far[1][:2])] if split else []
    due += [(g, near[1]) for g in range(groups - 1 if split else groups)]
    due += [(groups - 1, far[1][2:])] if split else []

    def pass_values(count):
        for g, rounds in due[:count]:
            pass_on(rounds, vbuf, 0, g)
        del due[:count]

    pass_values(1)
    gather(False)
    q_scale = scale_of(1)
    for i in range(heads):
        cols = slice(i * HD, (i + 1) * HD)
        scaled = q_raw[:, cols].astype(jnp.float32) * q_scale * q_gain[cols][None, :]
        queries[i // per, :, (i % per) * HD : (i % per + 1) * HD] = turned(scaled).astype(jnp.bfloat16)
    c_scale = scale_of(2)
    for i in range(heads):
        cols = slice(i * HD, (i + 1) * HD)
        cross[i // per, :, (i % per) * HD : (i % per + 1) * HD] = (
            c_raw[:, cols].astype(jnp.float32) * c_scale * c_gain[cols][None, :]
        ).astype(jnp.bfloat16)
    for r in range(txt // rows):
        t_scale = scale_of(3 + r)
        span = slice(r * rows, (r + 1) * rows)
        for i in range(heads):
            cols = slice(i * HD, (i + 1) * HD)
            texts[i // per, span, (i % per) * HD : (i % per + 1) * HD] = (
                t_raw[span, cols].astype(jnp.float32) * t_scale * t_gain[cols][None, :]
            ).astype(jnp.bfloat16)

    scale = 1.0 / math.sqrt(HD)

    def weigh(scores, dead):
        scores = jnp.where(dead > 0.5, BIG, scores * scale)
        highest = jnp.max(scores, axis=1, keepdims=True)
        weights = jnp.exp(scores - highest)
        total = jnp.sum(weights, axis=1, keepdims=True)
        return weights.astype(jnp.bfloat16), total

    def against(query, key):
        return lax.dot_general(query, key, (((1,), (1,)), ((), ())), preferred_element_type=jnp.float32)

    loads[4].wait()

    pass_values(1)
    dead_text = text_live[0:1, :]
    for i in range(heads):
        g, cols = i // per, slice((i % per) * HD, (i % per + 1) * HD)
        weights, total = weigh(against(cross[g, :, cols], texts[g, :, cols]), dead_text)
        mixed = jnp.dot(weights, t_val[:, i * HD : (i + 1) * HD], preferred_element_type=jnp.float32)
        text_out[g, :, cols] = mixed / total
        if i == heads // 2 - 1:
            pass_values(2)
    pass_values(len(due))
    if split:
        pass_on(far[1][:2], kbuf, 1, groups - 1)

    def self_group(which, rounds, g):
        pass_on(rounds, kbuf, 1, g)
        arrive(which, vbuf, 0, g)
        arrive(which, kbuf, 1, g)
        dead = live[0:1, :]
        for i in range(per):
            cols = slice(i * HD, (i + 1) * HD)
            query = queries[g, :, cols]
            scores = jnp.concatenate([against(query, kbuf[base + j, g, :, cols]) for j in range(SPAN)], axis=1)
            weights, total = weigh(scores, dead)
            mixed = jnp.zeros((rows, HD), jnp.float32)
            for j in range(SPAN):
                mixed = mixed + jnp.dot(
                    weights[:, j * rows : (j + 1) * rows], vbuf[base + j, g, :, cols], preferred_element_type=jnp.float32
                )
            at = pl.ds(pl.multiple_of(g * WIDE + i * HD, HD), HD)
            out_ref[:, at] = (mixed / total + text_out[g, :, cols]).astype(jnp.bfloat16)

    def near_group(g, carry):
        self_group(near, near[1], g)
        return carry

    def near_drain(g, carry):
        drain(near, vbuf, 0, g)
        drain(near, kbuf, 1, g)
        return carry

    lax.fori_loop(0, groups - 1 if split else groups, near_group, 0)
    if split:
        self_group(far, far[1][2:], groups - 1)
        drain(far, vbuf, 0, groups - 1)
        drain(far, kbuf, 1, groups - 1)
    lax.fori_loop(0, groups - 1 if split else groups, near_drain, 0)
    for first in (True, False):
        for o in range(1, SHARDS):
            share(o, shard, first).wait_send()


def rotary_tables(rows):
    positions = np.arange(SPAN * rows)
    spatial = HD // 6
    temporal = HD // 2 - 2 * spatial

    def rates(amount):
        return (1.0 / 10000.0 ** (np.arange(amount) / amount)).astype(np.float32)

    angle = np.concatenate(
        [
            (positions // (HGT * WID)).astype(np.float32)[:, None] * rates(temporal)[None, :],
            (positions // WID % HGT).astype(np.float32)[:, None] * rates(spatial)[None, :],
            (positions % WID).astype(np.float32)[:, None] * rates(spatial)[None, :],
        ],
        axis=1,
    ).astype(np.float64)
    cosine = np.repeat(np.cos(angle), 2, axis=1).astype(np.float32)
    sine = np.repeat(np.sin(angle), 2, axis=1).astype(np.float32)
    sine[:, 0::2] *= -1.0
    return cosine, sine


def fused(
    self_query, self_key, self_value, cross_query, text_key, text_value,
    query_gain, key_gain, cross_gain, text_gain, tile_item, row_count, text_len,
):
    rows, width = self_query.shape
    txt = text_key.shape[0]
    groups = width // WIDE
    cosine, sine = rotary_tables(rows)
    bf16, f32 = jnp.bfloat16, jnp.float32
    hbm = pl.BlockSpec(memory_space=pl.ANY)
    vmem = pl.BlockSpec(memory_space=pltpu.VMEM)

    def call(start):
        return pl.pallas_call(
            functools.partial(kernel, start),
            out_shape=jax.ShapeDtypeStruct((rows, width), bf16),
            in_specs=[hbm] * 15,
            out_specs=vmem,
            scratch_shapes=[pltpu.VMEM((width,), f32)] * 4
            + [pltpu.VMEM((SPAN * rows, HD), f32)] * 2
            + [pltpu.SMEM((TILES,), jnp.int32)] * 3
            + [
                pltpu.VMEM((rows, width), bf16),
                pltpu.VMEM((rows, width), bf16),
                pltpu.VMEM((rows, width), bf16),
                pltpu.VMEM((txt, width), bf16),
                pltpu.VMEM((txt, width), bf16),
                pltpu.VMEM((groups, rows, WIDE), bf16),
                pltpu.VMEM((groups, rows, WIDE), bf16),
                pltpu.VMEM((groups, txt, WIDE), bf16),
                pltpu.VMEM((groups, rows, WIDE), f32),
                pltpu.VMEM((TILES, groups, rows, WIDE), bf16),
                pltpu.VMEM((TILES, groups, rows, WIDE), bf16),
                pltpu.VMEM((SHARDS, 8, 3 * rows + txt), f32),
                pltpu.VMEM((8, SPAN * rows), f32),
                pltpu.VMEM((8, txt), f32),
                pltpu.SemaphoreType.DMA((14 + groups,)),
                pltpu.SemaphoreType.DMA((SHARDS - 1,)),
                pltpu.SemaphoreType.DMA((SHARDS,)),
                pltpu.SemaphoreType.DMA((SHARDS - 1,)),
                pltpu.SemaphoreType.DMA((SHARDS,)),
                pltpu.SemaphoreType.DMA((2, TILES, groups, 4)),
                pltpu.SemaphoreType.DMA((2, TILES, groups)),
            ],
            compiler_params=pltpu.CompilerParams(
                collective_id=start, has_side_effects=True, vmem_limit_bytes=40 * 1024 * 1024
            ),
        )

    operands = (
        self_query, self_key, self_value, cross_query, text_key, text_value,
        query_gain, key_gain, cross_gain, text_gain,
        jnp.asarray(cosine), jnp.asarray(sine), tile_item, row_count, text_len,
    )
    full = tile_item[SPAN - 1 :] == tile_item[: TILES - SPAN + 1]
    start = jnp.argmax(full).astype(jnp.int32)
    return lax.switch(start, [call(s) for s in range(TILES - SPAN + 1)], *operands)


def solution(mesh):
    in_specs = (
        P("tile", "head"),
        P("tile", "head"),
        P("tile", "head"),
        P("tile", "head"),
        P("tile", "head"),
        P("tile", "head"),
        P("head"),
        P("head"),
        P("head"),
        P("head"),
        P(),
        P(),
        P(),
    )
    out_specs = P("tile", "head")
    small = mesh.shape["tile"] == TILES and mesh.shape["head"] == SHARDS
    return jax.shard_map(
        fused if small else per_device, mesh=mesh, in_specs=in_specs, out_specs=out_specs, check_vma=False
    )
```

```python
import functools
import math

import jax
import jax.numpy as jnp
import numpy as np
from jax import lax
from jax.experimental import pallas as pl
from jax.experimental.pallas import tpu as pltpu
from jax.sharding import PartitionSpec as P

D = 5120
HD = 128
HGT = 30
WID = 52


EPSILON = 1e-06


def shifted(value, axis, by):
    peers = lax.axis_size(axis)
    pairs = [(i, i + by) for i in range(peers) if 0 <= i + by < peers]
    return lax.ppermute(value, axis, pairs)


def frequencies(amount, dimension):
    return 1.0 / 10000.0 ** (jnp.arange(amount, dtype=jnp.float32) * 2.0 / dimension)


def rope_angles(positions):
    spatial = HD // 6
    temporal = HD // 2 - 2 * spatial
    frame = (positions // (HGT * WID)).astype(jnp.float32)
    height = (positions // WID % HGT).astype(jnp.float32)
    across = (positions % WID).astype(jnp.float32)
    return jnp.concatenate(
        [
            frame[:, None] * frequencies(temporal, 2 * temporal)[None, :],
            height[:, None] * frequencies(spatial, 2 * spatial)[None, :],
            across[:, None] * frequencies(spatial, 2 * spatial)[None, :],
        ],
        axis=1,
    )


def pair_partner(matrix):
    index = jnp.arange(matrix.shape[-1])
    return jnp.where(index % 2 == 0, -jnp.roll(matrix, -1, axis=-1), jnp.roll(matrix, 1, axis=-1))


def rotate(matrix, angle):
    cosine = jnp.repeat(jnp.cos(angle), 2, axis=1)
    sine = jnp.repeat(jnp.sin(angle), 2, axis=1)
    shaped = matrix.reshape(matrix.shape[0], matrix.shape[1] // HD, HD)
    turned = shaped * cosine[:, None, :] + pair_partner(shaped) * sine[:, None, :]
    return turned.reshape(matrix.shape)


def scaled_rows(values, mean_square, gain):
    return values * lax.rsqrt(mean_square[:, None] + EPSILON) * gain[None, :]


def attend_head(query, key_rows, value_rows, live):
    scale = 1.0 / math.sqrt(HD)
    scores = (
        lax.dot_general(
            query, key_rows, (((1,), (1,)), ((), ())), preferred_element_type=jnp.float32
        )
        * scale
    )
    scores = jnp.where(live[None, :], scores, -1e30)
    highest = jnp.max(scores, axis=1, keepdims=True)
    weights = jnp.exp(scores - highest)
    total = jnp.sum(weights, axis=1, keepdims=True)
    mixed = jnp.dot(weights.astype(jnp.bfloat16), value_rows, preferred_element_type=jnp.float32)
    return mixed / total


def per_device(
    self_query,
    self_key,
    self_value,
    cross_query,
    text_key,
    text_value,
    query_gain,
    key_gain,
    cross_gain,
    text_gain,
    tile_item,
    row_count,
    text_len,
):
    row_total = self_query.shape[0]
    text_total = text_key.shape[0]
    head_total = self_query.shape[1] // HD
    tile_here = lax.axis_index("tile")
    tile_total = lax.axis_size("tile")
    span = min(7, tile_total // 2)
    item_here = tile_item[tile_here]
    first_tile = jnp.sum((tile_item < item_here).astype(jnp.int32))
    positions = (tile_here - first_tile) * row_total + jnp.arange(row_total, dtype=jnp.int32)
    angle = rope_angles(positions)
    query_float = self_query.astype(jnp.float32)
    key_float = self_key.astype(jnp.float32)
    cross_float = cross_query.astype(jnp.float32)
    text_float = text_key.astype(jnp.float32)
    query_sq, key_sq, cross_sq, text_sq = lax.psum(
        (
            jnp.sum(query_float * query_float, axis=1),
            jnp.sum(key_float * key_float, axis=1),
            jnp.sum(cross_float * cross_float, axis=1),
            jnp.sum(text_float * text_float, axis=1),
        ),
        "head",
    )
    queries = rotate(scaled_rows(query_float, query_sq / D, query_gain), angle).astype(jnp.bfloat16)
    rotated_keys = rotate(scaled_rows(key_float, key_sq / D, key_gain), angle).astype(jnp.bfloat16)
    cross = scaled_rows(cross_float, cross_sq / D, cross_gain).astype(jnp.bfloat16)
    texts = scaled_rows(text_float, text_sq / D, text_gain).astype(jnp.bfloat16)

    def live_rows(source):
        inside = (source >= 0) & (source < tile_total)
        clipped = jnp.clip(source, 0, tile_total - 1)
        same_item = inside & (tile_item[clipped] == item_here)
        return same_item & (jnp.arange(row_total, dtype=jnp.int32) < row_count[clipped])

    key_parts = [rotated_keys]
    value_parts = [self_value]
    live_parts = [live_rows(tile_here)]
    for distance in range(1, span):
        for offset in (distance, -distance):
            moved_keys, moved_values = shifted((rotated_keys, self_value), "tile", offset)
            key_parts.append(moved_keys)
            value_parts.append(moved_values)
            live_parts.append(live_rows(tile_here - offset))
    keys_all = jnp.concatenate(key_parts, axis=0)
    values_all = jnp.concatenate(value_parts, axis=0)
    live_all = jnp.concatenate(live_parts, axis=0)
    text_live = jnp.arange(text_total, dtype=jnp.int32) < text_len[item_here]

    def per_head(head_index):
        first_column = head_index * HD

        def columns(matrix):
            return lax.dynamic_slice_in_dim(matrix, first_column, HD, 1)

        local_part = attend_head(columns(queries), columns(keys_all), columns(values_all), live_all)
        text_part = attend_head(columns(cross), columns(texts), columns(text_value), text_live)
        return (local_part + text_part).astype(jnp.bfloat16)

    head_outputs = lax.map(per_head, jnp.arange(head_total, dtype=jnp.int32))
    return jnp.moveaxis(head_outputs, 0, 1).reshape(row_total, head_total * HD)


TILES = 8
SHARDS = 4
SPAN = 4
WIDE = 256
BIG = -1e30


def needs(start):
    found = []
    for t in range(TILES):
        if start <= t < start + SPAN:
            found.append({b for b in range(start, start + SPAN) if b != t})
        else:
            near = {t - 1, t + 1} & set(range(TILES))
            found.append({b for b in near if not start <= b < start + SPAN})
    return found


def window(start):
    return [start if start <= t < start + SPAN else (0 if t < start else TILES - SPAN) for t in range(TILES)]


def chip_edges(start, block, chips, far):
    if start > 2:
        return [(3 - a, 3 - c) for a, c in chip_edges(TILES - SPAN - start, TILES - 1 - block, {3 - c for c in chips}, far)]
    home = block // 2
    if start == 0 and block < SPAN and far:
        return [(0, 2), (2, 3), (3, 1)] if home == 0 else [(1, 3), (3, 2), (2, 0)]
    if start == 1 and block in (2, 3, 4):
        return {2: [(1, 0), (0, 2)], 3: [(1, 0), (1, 3), (3, 2)], 4: [(2, 0), (2, 3), (3, 1)]}[block]
    if start == 2 and 2 <= block <= 5:
        return {2: [(1, 0), (0, 2)], 3: [(1, 3), (3, 2)], 4: [(2, 3), (3, 1)], 5: [(2, 0), (0, 1)]}[block]
    return [(home, chip) for chip in sorted(chips)]


def edges_of(start, far):
    need = needs(start)
    edges = []
    for b in range(TILES):
        users = [t for t in range(TILES) if b in need[t]]
        home, core = b // 2, b % 2
        held = {home: (b, 0)}
        if b ^ 1 in users:
            edges.append((b, b ^ 1, b, 0))
        chips = {t // 2 for t in users} - {home}
        for a, c in chip_edges(start, b, chips, far):
            src, depth = held[a]
            same = 2 * c + core
            onward = any(x == c for x, _ in chip_edges(start, b, chips, far))
            entry = same if same in users or onward or same ^ 1 not in users else same ^ 1
            edges.append((src, entry, b, depth))
            held[c] = (entry, depth + 1)
            if entry ^ 1 in users:
                edges.append((entry, entry ^ 1, b, depth + 1))
    return edges


def plan_of(start, far):
    edges = edges_of(start, far)
    first = [[e[1] for e in sorted(edges) if e[3] == 0 and e[0] == t] for t in range(TILES)]
    first = [sorted(f, key=lambda v, t=t: v == t ^ 1) for t, f in enumerate(first)]
    rounds = []
    for depth in range(1, 1 + max([e[3] for e in edges])):
        events = []
        for t in range(TILES):
            mine = sorted({e[2] for e in edges if e[3] == depth and e[0] == t})
            dests = [(b, sorted([e[1] for e in edges if e[0] == t and e[2] == b], key=lambda v: v == t ^ 1)) for b in mine]
            events.append(dests)
        for k in range(max(len(e) for e in events)):
            rounds.append([e[k] if k < len(e) else None for e in events])
    gets = [{e[2] for e in edges if e[1] == t} for t in range(TILES)]
    passed = [{e[2] for e in edges if e[3] > 0 and e[0] == t} for t in range(TILES)]
    return first, rounds, gets, passed


def kernel(
    start,
    q_in, k_in, v_in, c_in, tk_in, tv_in,
    q_gain_in, k_gain_in, c_gain_in, t_gain_in,
    cos_in, sin_in, tile_item, row_count, text_len,
    out_ref,
    q_gain, k_gain, c_gain, t_gain,
    cos_ref, sin_ref,
    raw, t_val, scales, queries, text_out,
    kbuf, vbuf, sums, live, text_live,
    in_sem, y_send, y_recv, z_send, z_recv, send_sem, recv_sem,
):
    me = lax.axis_index("tile")
    shard = lax.axis_index("head")
    rows = q_in.shape[0]
    heads = q_in.shape[1] // HD
    groups = q_in.shape[1] // WIDE
    per = WIDE // HD
    txt = tk_in.shape[0]

    def pick(values):
        result = jnp.int32(values[0])
        for i in range(1, TILES):
            if values[i] != values[0]:
                result = jnp.where(me == i, jnp.int32(values[i]), result)
        return result

    loads = [
        pltpu.make_async_copy(src, dst, in_sem.at[i])
        for i, (src, dst) in enumerate(
            ((k_in, raw.at[0:rows]), (q_in, raw.at[rows : 2 * rows]), (c_in, raw.at[2 * rows : 3 * rows]),
             (tk_in, raw.at[3 * rows :]), (tv_in, t_val),
             (cos_in, cos_ref), (sin_in, sin_ref),
             (k_gain_in, k_gain), (q_gain_in, q_gain), (c_gain_in, c_gain), (t_gain_in, t_gain))
        )
    ]
    own = [
        pltpu.make_async_copy(v_in.at[:, g * WIDE : (g + 1) * WIDE], vbuf.at[me, g], in_sem.at[len(loads) + g])
        for g in range(groups)
    ]
    for load in own + loads:
        load.start()

    barrier = pltpu.get_barrier_semaphore()
    for o in range(1, TILES):
        pl.semaphore_signal(barrier, inc=1, device_id=(lax.rem(me + o, TILES), shard), device_id_type=pl.DeviceIdType.MESH)
    for o in range(1, SHARDS):
        pl.semaphore_signal(barrier, inc=1, device_id=(me, lax.rem(shard + o, SHARDS)), device_id_type=pl.DeviceIdType.MESH)
    pl.semaphore_wait(barrier, TILES + SHARDS - 2)

    near, far = plan_of(start, False), plan_of(start, True)
    split = start in (0, TILES - SPAN)
    shift = groups - 1 if split else 0
    base = pick(window(start))

    def plan(g):
        return far if split and g == groups - 1 else near

    def send(src, buf, kind, block, g, lane, dest):
        return pltpu.make_async_remote_copy(
            src_ref=src,
            dst_ref=buf.at[block, g],
            send_sem=send_sem.at[kind, block, g, lane],
            recv_sem=recv_sem.at[kind, block, g],
            device_id=(dest, shard),
            device_id_type=pl.DeviceIdType.MESH,
        )

    def each_first(g, act):
        firsts = [f[0] for f in ((near, far) if split else (near,))]
        for lane in range(max(len(f) for first in firsts for f in first)):
            lists = [[f[lane] if lane < len(f) else -1 for f in first] for first in firsts]
            dest = pick(lists[0])
            if lists[-1] != lists[0]:
                dest = jnp.where(g == groups - 1, pick(lists[-1]), dest)

            def run(lane=lane, dest=dest):
                act(lane, dest)

            if any(-1 in one for one in lists):
                pl.when(dest >= 0)(run)
            else:
                run()

    def each_round(rounds, act):
        for one in rounds:
            block = pick([e[0] if e else -1 for e in one])
            widest = max(len(e[1]) for e in one if e)
            dests = [pick([e[1][i] if e and i < len(e[1]) else -1 for e in one]) for i in range(widest)]

            def run(block=block, dests=dests):
                act(block, dests)

            if any(e is None for e in one):
                pl.when(block >= 0)(run)
            else:
                run()

    def pass_on(rounds, buf, kind, g):
        def act(block, dests):
            send(buf.at[block, g], buf, kind, block, g, 0, me).wait_recv()
            for lane, dest in enumerate(dests):

                def go(lane=lane, dest=dest):
                    send(buf.at[block, g], buf, kind, block, g, lane, dest).start()

                pl.when(dest >= 0)(go)

        each_round(rounds, act)

    def arrive(which, buf, kind, g):
        _, _, gets, passed = which
        for j in range(SPAN):
            waits = [int(window(start)[t] + j in gets[t] and window(start)[t] + j not in passed[t]) for t in range(TILES)]

            def go(j=j):
                send(buf.at[base + j, g], buf, kind, base + j, g, 0, me).wait_recv()

            if any(waits):
                pl.when(pick(waits) == 1)(go)

    def drain(which, buf, kind, g):
        def of_first(lane, dest):
            send(buf.at[me, g], buf, kind, me, g, lane, dest).wait_send()

        each_first(g, of_first)

        def of_round(block, dests):
            for lane, dest in enumerate(dests):

                def go(lane=lane, dest=dest):
                    send(buf.at[block, g], buf, kind, block, g, lane, dest).wait_send()

                pl.when(dest >= 0)(go)

        each_round(which[1], of_round)

    for load in own:
        load.wait()

    def give_value(i, carry):
        g = lax.rem(i + shift, groups)

        def of_value(lane, dest):
            send(vbuf.at[me, g], vbuf, 0, me, g, lane, dest).start()

        each_first(g, of_value)
        return carry

    lax.fori_loop(0, groups, give_value, 0)

    for which, g0, g1 in ((near, 0, groups - 1 if split else groups), (far, groups - 1, groups)):
        if g1 == groups and which is far and not split:
            continue
        for j in range(SPAN):
            empty = [int(window(start)[t] + j not in which[2][t] and window(start)[t] + j != t) for t in range(TILES)]
            if any(empty):

                @pl.when(pick(empty) == 1)
                def _(j=j, g0=g0, g1=g1):
                    for g in range(g0, g1):
                        vbuf[base + j, g] = jnp.zeros((rows, WIDE), jnp.bfloat16)

    def partial(i):
        span = pl.ds(pl.multiple_of(i * rows, rows), rows)
        total = jnp.zeros((rows, HD), jnp.float32)
        for c in range(heads):
            part = raw[span, c * HD : (c + 1) * HD].astype(jnp.float32)
            total = total + part * part
        column = jnp.sum(total, axis=1, keepdims=True)
        sums[shard, :, span] = jnp.broadcast_to(column, (rows, HD)).T[0:8, :]

    def share(o, slot, first):
        span = pl.ds(0, rows) if first else pl.ds(rows, 2 * rows + txt)
        return pltpu.make_async_remote_copy(
            src_ref=sums.at[slot, :, span],
            dst_ref=sums.at[slot, :, span],
            send_sem=(y_send if first else z_send).at[o - 1],
            recv_sem=(y_recv if first else z_recv).at[slot],
            device_id=(me, lax.rem(shard + o, SHARDS)),
            device_id_type=pl.DeviceIdType.MESH,
        )

    def gather(first):
        for o in range(1, SHARDS):
            share(o, lax.rem(shard + o, SHARDS), first).wait_recv()

    def other_sums(i, carry):
        partial(i)
        return carry

    loads[0].wait()
    partial(0)
    for o in range(1, SHARDS):
        share(o, shard, True).start()
    for load in loads[1:4]:
        load.wait()
    lax.fori_loop(1, 3 + txt // rows, other_sums, 0)
    for o in range(1, SHARDS):
        share(o, shard, False).start()

    for load in loads[5:]:
        load.wait()
    item = tile_item[me]
    before = jnp.int32(0)
    for t in range(TILES):
        before = before + jnp.where(tile_item[t] < item, 1, 0).astype(jnp.int32)
    place = me - before
    words = jnp.int32(0)
    for t in range(TILES):
        words = words + jnp.where(item == t, text_len[t], 0).astype(jnp.int32)
    lane_row = lax.broadcasted_iota(jnp.int32, (8, rows), 1)
    for j in range(SPAN):
        block = base + j
        limit = jnp.where(tile_item[block] == item, row_count[block], 0)
        live[:, j * rows : (j + 1) * rows] = jnp.where(lane_row < limit, 0.0, 1.0).astype(jnp.float32)
    lane_text = lax.broadcasted_iota(jnp.int32, (8, txt), 1)
    text_live[...] = jnp.where(lane_text < words, 0.0, 1.0).astype(jnp.float32)

    gather(True)

    def set_scale(i, carry):
        span = pl.ds(pl.multiple_of(i * rows, rows), rows)
        total = (sums[0, :, span] + sums[1, :, span]) + (sums[2, :, span] + sums[3, :, span])
        scale = lax.rsqrt(total / D + EPSILON)
        scales[span, :] = jnp.broadcast_to(scale[0:1, :], (HD, rows)).T
        return carry

    set_scale(0, 0)
    cosine = cos_ref[0:rows, :]
    sine = sin_ref[0:rows, :]
    for j in range(1, SPAN):
        cosine = jnp.where(place == j, cos_ref[j * rows : (j + 1) * rows, :], cosine)
        sine = jnp.where(place == j, sin_ref[j * rows : (j + 1) * rows, :], sine)
    even = lax.broadcasted_iota(jnp.int32, (rows, HD), 1) % 2 == 0

    def turned(values):
        partner = jnp.where(even, pltpu.roll(values, HD - 1, 1), pltpu.roll(values, 1, 1))
        return values * cosine + partner * sine

    def scaled(row, amount, head, gain):
        at = pl.ds(pl.multiple_of(head * HD, HD), HD)
        span = slice(row * rows, (row + amount) * rows)
        return raw[span, at].astype(jnp.float32) * scales[span, :] * gain[at][None, :]

    def give_key(i, carry):
        g = lax.rem(i + shift, groups)
        for p in range(per):
            kbuf[me, g, :, p * HD : (p + 1) * HD] = turned(scaled(0, 1, g * per + p, k_gain)).astype(jnp.bfloat16)

        def of_key(lane, dest):
            send(kbuf.at[me, g], kbuf, 1, me, g, lane, dest).start()

        each_first(g, of_key)
        return carry

    lax.fori_loop(0, groups, give_key, 0)

    if split:
        pass_on(far[1][:2], vbuf, 0, groups - 1)
    gather(False)
    lax.fori_loop(1, 3 + txt // rows, set_scale, 0)

    def set_query(g, carry):
        for p in range(per):
            queries[g, :, p * HD : (p + 1) * HD] = turned(scaled(1, 1, g * per + p, q_gain)).astype(jnp.bfloat16)
        return carry

    lax.fori_loop(0, groups, set_query, 0)

    scale = math.log2(math.e) / math.sqrt(HD)

    def weigh(scores, dead):
        scores = jnp.where(dead > 0.5, BIG, scores * scale)
        highest = jnp.max(scores, axis=1, keepdims=True)
        weights = jnp.exp2(scores - highest)
        total = jnp.sum(weights, axis=1, keepdims=True)
        return weights.astype(jnp.bfloat16), total

    def against(query, key):
        return lax.dot_general(query, key, (((1,), (1,)), ((), ())), preferred_element_type=jnp.float32)

    loads[4].wait()

    def text_group(g, carry):
        dead = text_live[0:1, :]
        for p in range(per):
            cols = slice(p * HD, (p + 1) * HD)
            head = g * per + p
            query = scaled(2, 1, head, c_gain).astype(jnp.bfloat16)
            words_here = scaled(3, txt // rows, head, t_gain).astype(jnp.bfloat16)
            weights, total = weigh(against(query, words_here), dead)
            at = pl.ds(pl.multiple_of(head * HD, HD), HD)
            text_out[g, :, cols] = jnp.dot(weights, t_val[:, at], preferred_element_type=jnp.float32) / total
        if split:

            @pl.when(g < groups - 1)
            def _():
                pass_on(near[1], vbuf, 0, g)

        else:
            pass_on(near[1], vbuf, 0, g)
        return carry

    lax.fori_loop(0, groups, text_group, 0)
    if split:
        pass_on(far[1][:2], kbuf, 1, groups - 1)
        pass_on(far[1][2:], vbuf, 0, groups - 1)

    def self_group(which, rounds, g):
        pass_on(rounds, kbuf, 1, g)
        arrive(which, vbuf, 0, g)
        arrive(which, kbuf, 1, g)
        dead = live[0:1, :]
        for i in range(per):
            cols = slice(i * HD, (i + 1) * HD)
            query = queries[g, :, cols]
            keys = kbuf[pl.ds(base, SPAN), g, :, cols].reshape(SPAN * rows, HD)
            values = vbuf[pl.ds(base, SPAN), g, :, cols].reshape(SPAN * rows, HD)
            weights, total = weigh(against(query, keys), dead)
            mixed = jnp.dot(weights, values, preferred_element_type=jnp.float32)
            at = pl.ds(pl.multiple_of(g * WIDE + i * HD, HD), HD)
            out_ref[:, at] = (mixed / total + text_out[g, :, cols]).astype(jnp.bfloat16)

    def near_group(g, carry):
        self_group(near, near[1], g)
        return carry

    def near_drain(g, carry):
        drain(near, vbuf, 0, g)
        drain(near, kbuf, 1, g)
        return carry

    lax.fori_loop(0, groups - 1 if split else groups, near_group, 0)
    if split:
        self_group(far, far[1][2:], groups - 1)
        drain(far, vbuf, 0, groups - 1)
        drain(far, kbuf, 1, groups - 1)
    lax.fori_loop(0, groups - 1 if split else groups, near_drain, 0)
    for first in (True, False):
        for o in range(1, SHARDS):
            share(o, shard, first).wait_send()


def rotary_tables(rows):
    positions = np.arange(SPAN * rows)
    spatial = HD // 6
    temporal = HD // 2 - 2 * spatial

    def rates(amount):
        return (1.0 / 10000.0 ** (np.arange(amount) / amount)).astype(np.float32)

    angle = np.concatenate(
        [
            (positions // (HGT * WID)).astype(np.float32)[:, None] * rates(temporal)[None, :],
            (positions // WID % HGT).astype(np.float32)[:, None] * rates(spatial)[None, :],
            (positions % WID).astype(np.float32)[:, None] * rates(spatial)[None, :],
        ],
        axis=1,
    ).astype(np.float64)
    cosine = np.repeat(np.cos(angle), 2, axis=1).astype(np.float32)
    sine = np.repeat(np.sin(angle), 2, axis=1).astype(np.float32)
    sine[:, 0::2] *= -1.0
    return cosine, sine


def fused(
    self_query, self_key, self_value, cross_query, text_key, text_value,
    query_gain, key_gain, cross_gain, text_gain, tile_item, row_count, text_len,
):
    rows, width = self_query.shape
    txt = text_key.shape[0]
    groups = width // WIDE
    cosine, sine = rotary_tables(rows)
    bf16, f32 = jnp.bfloat16, jnp.float32
    hbm = pl.BlockSpec(memory_space=pltpu.HBM)
    vmem = pl.BlockSpec(memory_space=pltpu.VMEM)
    smem = pl.BlockSpec(memory_space=pltpu.SMEM)

    def call(start):
        return pl.pallas_call(
            functools.partial(kernel, start),
            out_shape=jax.ShapeDtypeStruct((rows, width), bf16),
            in_specs=[hbm] * 12 + [smem] * 3,
            out_specs=vmem,
            scratch_shapes=[pltpu.VMEM((width,), f32)] * 4
            + [pltpu.VMEM((SPAN * rows, HD), f32)] * 2
            + [
                pltpu.VMEM((3 * rows + txt, width), bf16),
                pltpu.VMEM((txt, width), bf16),
                pltpu.VMEM((3 * rows + txt, HD), f32),
                pltpu.VMEM((groups, rows, WIDE), bf16),
                pltpu.VMEM((groups, rows, WIDE), f32),
                pltpu.VMEM((TILES, groups, rows, WIDE), bf16),
                pltpu.VMEM((TILES, groups, rows, WIDE), bf16),
                pltpu.VMEM((SHARDS, 8, 3 * rows + txt), f32),
                pltpu.VMEM((8, SPAN * rows), f32),
                pltpu.VMEM((8, txt), f32),
                pltpu.SemaphoreType.DMA((11 + groups,)),
                pltpu.SemaphoreType.DMA((SHARDS - 1,)),
                pltpu.SemaphoreType.DMA((SHARDS,)),
                pltpu.SemaphoreType.DMA((SHARDS - 1,)),
                pltpu.SemaphoreType.DMA((SHARDS,)),
                pltpu.SemaphoreType.DMA((2, TILES, groups, 4)),
                pltpu.SemaphoreType.DMA((2, TILES, groups)),
            ],
            compiler_params=pltpu.CompilerParams(
                collective_id=start, has_side_effects=True, vmem_limit_bytes=40 * 1024 * 1024
            ),
        )

    operands = (
        self_query, self_key, self_value, cross_query, text_key, text_value,
        query_gain, key_gain, cross_gain, text_gain,
        jnp.asarray(cosine), jnp.asarray(sine), tile_item, row_count, text_len,
    )
    full = tile_item[SPAN - 1 :] == tile_item[: TILES - SPAN + 1]
    start = jnp.argmax(full).astype(jnp.int32)
    return lax.switch(start, [call(s) for s in range(TILES - SPAN + 1)], *operands)


def solution(mesh):
    in_specs = (
        P("tile", "head"),
        P("tile", "head"),
        P("tile", "head"),
        P("tile", "head"),
        P("tile", "head"),
        P("tile", "head"),
        P("head"),
        P("head"),
        P("head"),
        P("head"),
        P(),
        P(),
        P(),
    )
    out_specs = P("tile", "head")
    small = mesh.shape["tile"] == TILES and mesh.shape["head"] == SHARDS
    return jax.shard_map(
        fused if small else per_device, mesh=mesh, in_specs=in_specs, out_specs=out_specs, check_vma=False
    )
```

```python
import functools
import math

import jax
import jax.numpy as jnp
import numpy as np
from jax import lax
from jax.experimental import pallas as pl
from jax.experimental.pallas import tpu as pltpu
from jax.sharding import PartitionSpec as P

D = 5120
HD = 128
HGT = 30
WID = 52


EPSILON = 1e-06


def shifted(value, axis, by):
    peers = lax.axis_size(axis)
    pairs = [(i, i + by) for i in range(peers) if 0 <= i + by < peers]
    return lax.ppermute(value, axis, pairs)


def frequencies(amount, dimension):
    return 1.0 / 10000.0 ** (jnp.arange(amount, dtype=jnp.float32) * 2.0 / dimension)


def rope_angles(positions):
    spatial = HD // 6
    temporal = HD // 2 - 2 * spatial
    frame = (positions // (HGT * WID)).astype(jnp.float32)
    height = (positions // WID % HGT).astype(jnp.float32)
    across = (positions % WID).astype(jnp.float32)
    return jnp.concatenate(
        [
            frame[:, None] * frequencies(temporal, 2 * temporal)[None, :],
            height[:, None] * frequencies(spatial, 2 * spatial)[None, :],
            across[:, None] * frequencies(spatial, 2 * spatial)[None, :],
        ],
        axis=1,
    )


def pair_partner(matrix):
    index = jnp.arange(matrix.shape[-1])
    return jnp.where(index % 2 == 0, -jnp.roll(matrix, -1, axis=-1), jnp.roll(matrix, 1, axis=-1))


def rotate(matrix, angle):
    cosine = jnp.repeat(jnp.cos(angle), 2, axis=1)
    sine = jnp.repeat(jnp.sin(angle), 2, axis=1)
    shaped = matrix.reshape(matrix.shape[0], matrix.shape[1] // HD, HD)
    turned = shaped * cosine[:, None, :] + pair_partner(shaped) * sine[:, None, :]
    return turned.reshape(matrix.shape)


def scaled_rows(values, mean_square, gain):
    return values * lax.rsqrt(mean_square[:, None] + EPSILON) * gain[None, :]


def attend_head(query, key_rows, value_rows, live):
    scale = 1.0 / math.sqrt(HD)
    scores = (
        lax.dot_general(
            query, key_rows, (((1,), (1,)), ((), ())), preferred_element_type=jnp.float32
        )
        * scale
    )
    scores = jnp.where(live[None, :], scores, -1e30)
    highest = jnp.max(scores, axis=1, keepdims=True)
    weights = jnp.exp(scores - highest)
    total = jnp.sum(weights, axis=1, keepdims=True)
    mixed = jnp.dot(weights.astype(jnp.bfloat16), value_rows, preferred_element_type=jnp.float32)
    return mixed / total


def per_device(
    self_query,
    self_key,
    self_value,
    cross_query,
    text_key,
    text_value,
    query_gain,
    key_gain,
    cross_gain,
    text_gain,
    tile_item,
    row_count,
    text_len,
):
    row_total = self_query.shape[0]
    text_total = text_key.shape[0]
    head_total = self_query.shape[1] // HD
    tile_here = lax.axis_index("tile")
    tile_total = lax.axis_size("tile")
    span = min(7, tile_total // 2)
    item_here = tile_item[tile_here]
    first_tile = jnp.sum((tile_item < item_here).astype(jnp.int32))
    positions = (tile_here - first_tile) * row_total + jnp.arange(row_total, dtype=jnp.int32)
    angle = rope_angles(positions)
    query_float = self_query.astype(jnp.float32)
    key_float = self_key.astype(jnp.float32)
    cross_float = cross_query.astype(jnp.float32)
    text_float = text_key.astype(jnp.float32)
    query_sq, key_sq, cross_sq, text_sq = lax.psum(
        (
            jnp.sum(query_float * query_float, axis=1),
            jnp.sum(key_float * key_float, axis=1),
            jnp.sum(cross_float * cross_float, axis=1),
            jnp.sum(text_float * text_float, axis=1),
        ),
        "head",
    )
    queries = rotate(scaled_rows(query_float, query_sq / D, query_gain), angle).astype(jnp.bfloat16)
    rotated_keys = rotate(scaled_rows(key_float, key_sq / D, key_gain), angle).astype(jnp.bfloat16)
    cross = scaled_rows(cross_float, cross_sq / D, cross_gain).astype(jnp.bfloat16)
    texts = scaled_rows(text_float, text_sq / D, text_gain).astype(jnp.bfloat16)

    def live_rows(source):
        inside = (source >= 0) & (source < tile_total)
        clipped = jnp.clip(source, 0, tile_total - 1)
        same_item = inside & (tile_item[clipped] == item_here)
        return same_item & (jnp.arange(row_total, dtype=jnp.int32) < row_count[clipped])

    key_parts = [rotated_keys]
    value_parts = [self_value]
    live_parts = [live_rows(tile_here)]
    for distance in range(1, span):
        for offset in (distance, -distance):
            moved_keys, moved_values = shifted((rotated_keys, self_value), "tile", offset)
            key_parts.append(moved_keys)
            value_parts.append(moved_values)
            live_parts.append(live_rows(tile_here - offset))
    keys_all = jnp.concatenate(key_parts, axis=0)
    values_all = jnp.concatenate(value_parts, axis=0)
    live_all = jnp.concatenate(live_parts, axis=0)
    text_live = jnp.arange(text_total, dtype=jnp.int32) < text_len[item_here]

    def per_head(head_index):
        first_column = head_index * HD

        def columns(matrix):
            return lax.dynamic_slice_in_dim(matrix, first_column, HD, 1)

        local_part = attend_head(columns(queries), columns(keys_all), columns(values_all), live_all)
        text_part = attend_head(columns(cross), columns(texts), columns(text_value), text_live)
        return (local_part + text_part).astype(jnp.bfloat16)

    head_outputs = lax.map(per_head, jnp.arange(head_total, dtype=jnp.int32))
    return jnp.moveaxis(head_outputs, 0, 1).reshape(row_total, head_total * HD)


TILES = 8
SHARDS = 4
SPAN = 4
WIDE = 256
BIG = -1e30
LONG_WAY = False


def needs(start):
    found = []
    for t in range(TILES):
        if start <= t < start + SPAN:
            found.append({b for b in range(start, start + SPAN) if b != t})
        else:
            near = {t - 1, t + 1} & set(range(TILES))
            found.append({b for b in near if not start <= b < start + SPAN})
    return found


def window(start):
    return [start if start <= t < start + SPAN else (0 if t < start else TILES - SPAN) for t in range(TILES)]


def chip_edges(start, block, chips, far):
    if start > 2:
        return [(3 - a, 3 - c) for a, c in chip_edges(TILES - SPAN - start, TILES - 1 - block, {3 - c for c in chips}, far)]
    home = block // 2
    if start == 0 and block < SPAN and far:
        return [(0, 2), (2, 3), (3, 1)] if home == 0 else [(1, 3), (3, 2), (2, 0)]
    if start == 1 and block in (2, 3, 4):
        return {2: [(1, 0), (0, 2)], 3: [(1, 0), (1, 3), (3, 2)], 4: [(2, 0), (2, 3), (3, 1)]}[block]
    if start == 2 and 2 <= block <= 5:
        return {2: [(1, 0), (0, 2)], 3: [(1, 3), (3, 2)], 4: [(2, 3), (3, 1)], 5: [(2, 0), (0, 1)]}[block]
    return [(home, chip) for chip in sorted(chips)]


def edges_of(start, far):
    need = needs(start)
    edges = []
    for b in range(TILES):
        users = [t for t in range(TILES) if b in need[t]]
        home, core = b // 2, b % 2
        held = {home: (b, 0)}
        if b ^ 1 in users:
            edges.append((b, b ^ 1, b, 0))
        chips = {t // 2 for t in users} - {home}
        for a, c in chip_edges(start, b, chips, far):
            src, depth = held[a]
            same = 2 * c + core
            onward = any(x == c for x, _ in chip_edges(start, b, chips, far))
            entry = same if same in users or onward or same ^ 1 not in users else same ^ 1
            edges.append((src, entry, b, depth))
            held[c] = (entry, depth + 1)
            if entry ^ 1 in users:
                edges.append((entry, entry ^ 1, b, depth + 1))
    return edges


def plan_of(start, far):
    edges = edges_of(start, far)
    first = [[e[1] for e in sorted(edges) if e[3] == 0 and e[0] == t] for t in range(TILES)]
    first = [sorted(f, key=lambda v, t=t: v == t ^ 1) for t, f in enumerate(first)]
    rounds = []
    for depth in range(1, 1 + max([e[3] for e in edges])):
        events = []
        for t in range(TILES):
            mine = sorted({e[2] for e in edges if e[3] == depth and e[0] == t})
            dests = [(b, sorted([e[1] for e in edges if e[0] == t and e[2] == b], key=lambda v: v == t ^ 1)) for b in mine]
            events.append(dests)
        for k in range(max(len(e) for e in events)):
            rounds.append([e[k] if k < len(e) else None for e in events])
    gets = [{e[2] for e in edges if e[1] == t} for t in range(TILES)]
    passed = [{e[2] for e in edges if e[3] > 0 and e[0] == t} for t in range(TILES)]
    return first, rounds, gets, passed


def kernel(
    start,
    q_in, k_in, v_in, c_in, tk_in, tv_in,
    q_gain_in, k_gain_in, c_gain_in, t_gain_in,
    cos_in, sin_in, tile_item, row_count, text_len,
    out_ref,
    q_gain, k_gain, c_gain, t_gain,
    cos_ref, sin_ref,
    raw, t_val, scales, queries, text_out,
    kbuf, vbuf, sums, live, text_live,
    in_sem, y_send, y_recv, z_send, z_recv, send_sem, recv_sem,
):
    me = lax.axis_index("tile")
    shard = lax.axis_index("head")
    rows = q_in.shape[0]
    heads = q_in.shape[1] // HD
    groups = q_in.shape[1] // WIDE
    per = WIDE // HD
    txt = tk_in.shape[0]

    def pick(values):
        result = jnp.int32(values[0])
        for i in range(1, TILES):
            if values[i] != values[0]:
                result = jnp.where(me == i, jnp.int32(values[i]), result)
        return result

    loads = [
        pltpu.make_async_copy(src, dst, in_sem.at[i])
        for i, (src, dst) in enumerate(
            ((k_in, raw.at[0:rows]), (q_in, raw.at[rows : 2 * rows]), (c_in, raw.at[2 * rows : 3 * rows]),
             (tk_in, raw.at[3 * rows :]), (tv_in, t_val),
             (cos_in, cos_ref), (sin_in, sin_ref),
             (k_gain_in, k_gain), (q_gain_in, q_gain), (c_gain_in, c_gain), (t_gain_in, t_gain))
        )
    ]
    own = [
        pltpu.make_async_copy(v_in.at[:, g * WIDE : (g + 1) * WIDE], vbuf.at[me, g], in_sem.at[len(loads) + g])
        for g in range(groups)
    ]
    for load in own + loads:
        load.start()

    barrier = pltpu.get_barrier_semaphore()
    for o in range(1, TILES):
        pl.semaphore_signal(barrier, inc=1, device_id=(lax.rem(me + o, TILES), shard), device_id_type=pl.DeviceIdType.MESH)
    for o in range(1, SHARDS):
        pl.semaphore_signal(barrier, inc=1, device_id=(me, lax.rem(shard + o, SHARDS)), device_id_type=pl.DeviceIdType.MESH)
    pl.semaphore_wait(barrier, TILES + SHARDS - 2)

    near, far = plan_of(start, False), plan_of(start, True)
    split = LONG_WAY and start in (0, TILES - SPAN)
    shift = groups - 1 if split else 0
    base = pick(window(start))

    def plan(g):
        return far if split and g == groups - 1 else near

    def send(src, buf, kind, block, g, lane, dest):
        return pltpu.make_async_remote_copy(
            src_ref=src,
            dst_ref=buf.at[block, g],
            send_sem=send_sem.at[kind, block, g, lane],
            recv_sem=recv_sem.at[kind, block, g],
            device_id=(dest, shard),
            device_id_type=pl.DeviceIdType.MESH,
        )

    def each_first(g, act):
        firsts = [f[0] for f in ((near, far) if split else (near,))]
        for lane in range(max(len(f) for first in firsts for f in first)):
            lists = [[f[lane] if lane < len(f) else -1 for f in first] for first in firsts]
            dest = pick(lists[0])
            if lists[-1] != lists[0]:
                dest = jnp.where(g == groups - 1, pick(lists[-1]), dest)

            def run(lane=lane, dest=dest):
                act(lane, dest)

            if any(-1 in one for one in lists):
                pl.when(dest >= 0)(run)
            else:
                run()

    def each_round(rounds, act):
        for one in rounds:
            block = pick([e[0] if e else -1 for e in one])
            widest = max(len(e[1]) for e in one if e)
            dests = [pick([e[1][i] if e and i < len(e[1]) else -1 for e in one]) for i in range(widest)]

            def run(block=block, dests=dests):
                act(block, dests)

            if any(e is None for e in one):
                pl.when(block >= 0)(run)
            else:
                run()

    def pass_on(rounds, buf, kind, g):
        def act(block, dests):
            send(buf.at[block, g], buf, kind, block, g, 0, me).wait_recv()
            for lane, dest in enumerate(dests):

                def go(lane=lane, dest=dest):
                    send(buf.at[block, g], buf, kind, block, g, lane, dest).start()

                pl.when(dest >= 0)(go)

        each_round(rounds, act)

    def arrive(which, buf, kind, g):
        _, _, gets, passed = which
        for j in range(SPAN):
            waits = [int(window(start)[t] + j in gets[t] and window(start)[t] + j not in passed[t]) for t in range(TILES)]

            def go(j=j):
                send(buf.at[base + j, g], buf, kind, base + j, g, 0, me).wait_recv()

            if any(waits):
                pl.when(pick(waits) == 1)(go)

    def drain(which, buf, kind, g):
        def of_first(lane, dest):
            send(buf.at[me, g], buf, kind, me, g, lane, dest).wait_send()

        each_first(g, of_first)

        def of_round(block, dests):
            for lane, dest in enumerate(dests):

                def go(lane=lane, dest=dest):
                    send(buf.at[block, g], buf, kind, block, g, lane, dest).wait_send()

                pl.when(dest >= 0)(go)

        each_round(which[1], of_round)

    for load in own:
        load.wait()

    def give_value(i, carry):
        g = lax.rem(i + shift, groups)

        def of_value(lane, dest):
            send(vbuf.at[me, g], vbuf, 0, me, g, lane, dest).start()

        each_first(g, of_value)
        return carry

    lax.fori_loop(0, groups, give_value, 0)

    for which, g0, g1 in ((near, 0, groups - 1 if split else groups), (far, groups - 1, groups)):
        if g1 == groups and which is far and not split:
            continue
        for j in range(SPAN):
            empty = [int(window(start)[t] + j not in which[2][t] and window(start)[t] + j != t) for t in range(TILES)]
            if any(empty):

                @pl.when(pick(empty) == 1)
                def _(j=j, g0=g0, g1=g1):
                    for g in range(g0, g1):
                        vbuf[base + j, g] = jnp.zeros((rows, WIDE), jnp.bfloat16)

    def partial(i):
        span = pl.ds(pl.multiple_of(i * rows, rows), rows)
        total = jnp.zeros((rows, HD), jnp.float32)
        for c in range(heads):
            part = raw[span, c * HD : (c + 1) * HD].astype(jnp.float32)
            total = total + part * part
        column = jnp.sum(total, axis=1, keepdims=True)
        sums[shard, :, span] = jnp.broadcast_to(column, (rows, HD)).T[0:8, :]

    def share(o, slot, first):
        span = pl.ds(0, rows) if first else pl.ds(rows, 2 * rows + txt)
        return pltpu.make_async_remote_copy(
            src_ref=sums.at[slot, :, span],
            dst_ref=sums.at[slot, :, span],
            send_sem=(y_send if first else z_send).at[o - 1],
            recv_sem=(y_recv if first else z_recv).at[slot],
            device_id=(me, lax.rem(shard + o, SHARDS)),
            device_id_type=pl.DeviceIdType.MESH,
        )

    def gather(first):
        for o in range(1, SHARDS):
            share(o, lax.rem(shard + o, SHARDS), first).wait_recv()

    def other_sums(i, carry):
        partial(i)
        return carry

    loads[0].wait()
    partial(0)
    for o in range(1, SHARDS):
        share(o, shard, True).start()
    for load in loads[1:4]:
        load.wait()
    lax.fori_loop(1, 3 + txt // rows, other_sums, 0)
    for o in range(1, SHARDS):
        share(o, shard, False).start()

    for load in loads[5:]:
        load.wait()
    item = tile_item[me]
    before = jnp.int32(0)
    for t in range(TILES):
        before = before + jnp.where(tile_item[t] < item, 1, 0).astype(jnp.int32)
    place = me - before
    words = jnp.int32(0)
    for t in range(TILES):
        words = words + jnp.where(item == t, text_len[t], 0).astype(jnp.int32)
    lane_row = lax.broadcasted_iota(jnp.int32, (8, rows), 1)
    for j in range(SPAN):
        block = base + j
        limit = jnp.where(tile_item[block] == item, row_count[block], 0)
        live[:, j * rows : (j + 1) * rows] = jnp.where(lane_row < limit, 0.0, 1.0).astype(jnp.float32)
    lane_text = lax.broadcasted_iota(jnp.int32, (8, txt), 1)
    text_live[...] = jnp.where(lane_text < words, 0.0, 1.0).astype(jnp.float32)

    gather(True)

    def set_scale(i, carry):
        span = pl.ds(pl.multiple_of(i * rows, rows), rows)
        total = (sums[0, :, span] + sums[1, :, span]) + (sums[2, :, span] + sums[3, :, span])
        scale = lax.rsqrt(total / D + EPSILON)
        scales[span, :] = jnp.broadcast_to(scale[0:1, :], (HD, rows)).T
        return carry

    set_scale(0, 0)
    cosine = cos_ref[0:rows, :]
    sine = sin_ref[0:rows, :]
    for j in range(1, SPAN):
        cosine = jnp.where(place == j, cos_ref[j * rows : (j + 1) * rows, :], cosine)
        sine = jnp.where(place == j, sin_ref[j * rows : (j + 1) * rows, :], sine)
    even = lax.broadcasted_iota(jnp.int32, (rows, HD), 1) % 2 == 0

    def turned(values):
        partner = jnp.where(even, pltpu.roll(values, HD - 1, 1), pltpu.roll(values, 1, 1))
        return values * cosine + partner * sine

    def scaled(row, amount, head, gain):
        at = pl.ds(pl.multiple_of(head * HD, HD), HD)
        span = slice(row * rows, (row + amount) * rows)
        return raw[span, at].astype(jnp.float32) * scales[span, :] * gain[at][None, :]

    def give_key(i, carry):
        g = lax.rem(i + shift, groups)
        for p in range(per):
            kbuf[me, g, :, p * HD : (p + 1) * HD] = turned(scaled(0, 1, g * per + p, k_gain)).astype(jnp.bfloat16)

        def of_key(lane, dest):
            send(kbuf.at[me, g], kbuf, 1, me, g, lane, dest).start()

        each_first(g, of_key)
        return carry

    lax.fori_loop(0, groups, give_key, 0)

    if split:
        pass_on(far[1][:2], vbuf, 0, groups - 1)
    gather(False)
    lax.fori_loop(1, 3 + txt // rows, set_scale, 0)

    def set_query(g, carry):
        for p in range(per):
            queries[g, :, p * HD : (p + 1) * HD] = turned(scaled(1, 1, g * per + p, q_gain)).astype(jnp.bfloat16)
        return carry

    lax.fori_loop(0, groups, set_query, 0)

    scale = math.log2(math.e) / math.sqrt(HD)

    def weigh(scores, dead):
        scores = jnp.where(dead > 0.5, BIG, scores * scale)
        highest = jnp.max(scores, axis=1, keepdims=True)
        weights = jnp.exp2(scores - highest)
        total = jnp.sum(weights, axis=1, keepdims=True)
        return weights.astype(jnp.bfloat16), total

    def against(query, key):
        return lax.dot_general(query, key, (((1,), (1,)), ((), ())), preferred_element_type=jnp.float32)

    loads[4].wait()

    def text_group(g, carry):
        dead = text_live[0:1, :]
        for p in range(per):
            cols = slice(p * HD, (p + 1) * HD)
            head = g * per + p
            query = scaled(2, 1, head, c_gain).astype(jnp.bfloat16)
            words_here = scaled(3, txt // rows, head, t_gain).astype(jnp.bfloat16)
            weights, total = weigh(against(query, words_here), dead)
            at = pl.ds(pl.multiple_of(head * HD, HD), HD)
            text_out[g, :, cols] = jnp.dot(weights, t_val[:, at], preferred_element_type=jnp.float32) / total
        if split:

            @pl.when(g < groups - 1)
            def _():
                pass_on(near[1], vbuf, 0, g)

        else:
            pass_on(near[1], vbuf, 0, g)
        return carry

    lax.fori_loop(0, groups, text_group, 0)
    if split:
        pass_on(far[1][:2], kbuf, 1, groups - 1)
        pass_on(far[1][2:], vbuf, 0, groups - 1)

    def self_group(which, g):
        arrive(which, vbuf, 0, g)
        arrive(which, kbuf, 1, g)
        dead = live[0:1, :]
        for i in range(per):
            cols = slice(i * HD, (i + 1) * HD)
            query = queries[g, :, cols]
            keys = kbuf[pl.ds(base, SPAN), g, :, cols].reshape(SPAN * rows, HD)
            values = vbuf[pl.ds(base, SPAN), g, :, cols].reshape(SPAN * rows, HD)
            weights, total = weigh(against(query, keys), dead)
            mixed = jnp.dot(weights, values, preferred_element_type=jnp.float32)
            at = pl.ds(pl.multiple_of(g * WIDE + i * HD, HD), HD)
            out_ref[:, at] = (mixed / total + text_out[g, :, cols]).astype(jnp.bfloat16)

    last = groups - 1 - split

    def near_group(g, carry):
        @pl.when(g < last)
        def _():
            pass_on(near[1], kbuf, 1, g + 1)

        self_group(near, g)
        return carry

    pass_on(near[1], kbuf, 1, 0)
    def near_drain(g, carry):
        drain(near, vbuf, 0, g)
        drain(near, kbuf, 1, g)
        return carry

    lax.fori_loop(0, last, near_group, 0)
    if split:
        pass_on(far[1][2:], kbuf, 1, groups - 1)
    near_group(last, 0)
    if split:
        self_group(far, groups - 1)
        drain(far, vbuf, 0, groups - 1)
        drain(far, kbuf, 1, groups - 1)
    lax.fori_loop(0, groups - 1 if split else groups, near_drain, 0)
    for first in (True, False):
        for o in range(1, SHARDS):
            share(o, shard, first).wait_send()


def rotary_tables(rows):
    positions = np.arange(SPAN * rows)
    spatial = HD // 6
    temporal = HD // 2 - 2 * spatial

    def rates(amount):
        return (1.0 / 10000.0 ** (np.arange(amount) / amount)).astype(np.float32)

    angle = np.concatenate(
        [
            (positions // (HGT * WID)).astype(np.float32)[:, None] * rates(temporal)[None, :],
            (positions // WID % HGT).astype(np.float32)[:, None] * rates(spatial)[None, :],
            (positions % WID).astype(np.float32)[:, None] * rates(spatial)[None, :],
        ],
        axis=1,
    ).astype(np.float64)
    cosine = np.repeat(np.cos(angle), 2, axis=1).astype(np.float32)
    sine = np.repeat(np.sin(angle), 2, axis=1).astype(np.float32)
    sine[:, 0::2] *= -1.0
    return cosine, sine


def fused(
    self_query, self_key, self_value, cross_query, text_key, text_value,
    query_gain, key_gain, cross_gain, text_gain, tile_item, row_count, text_len,
):
    rows, width = self_query.shape
    txt = text_key.shape[0]
    groups = width // WIDE
    cosine, sine = rotary_tables(rows)
    bf16, f32 = jnp.bfloat16, jnp.float32
    hbm = pl.BlockSpec(memory_space=pltpu.HBM)
    vmem = pl.BlockSpec(memory_space=pltpu.VMEM)
    smem = pl.BlockSpec(memory_space=pltpu.SMEM)

    def call(start):
        return pl.pallas_call(
            functools.partial(kernel, start),
            out_shape=jax.ShapeDtypeStruct((rows, width), bf16),
            in_specs=[hbm] * 12 + [smem] * 3,
            out_specs=vmem,
            scratch_shapes=[pltpu.VMEM((width,), f32)] * 4
            + [pltpu.VMEM((SPAN * rows, HD), f32)] * 2
            + [
                pltpu.VMEM((3 * rows + txt, width), bf16),
                pltpu.VMEM((txt, width), bf16),
                pltpu.VMEM((3 * rows + txt, HD), f32),
                pltpu.VMEM((groups, rows, WIDE), bf16),
                pltpu.VMEM((groups, rows, WIDE), f32),
                pltpu.VMEM((TILES, groups, rows, WIDE), bf16),
                pltpu.VMEM((TILES, groups, rows, WIDE), bf16),
                pltpu.VMEM((SHARDS, 8, 3 * rows + txt), f32),
                pltpu.VMEM((8, SPAN * rows), f32),
                pltpu.VMEM((8, txt), f32),
                pltpu.SemaphoreType.DMA((11 + groups,)),
                pltpu.SemaphoreType.DMA((SHARDS - 1,)),
                pltpu.SemaphoreType.DMA((SHARDS,)),
                pltpu.SemaphoreType.DMA((SHARDS - 1,)),
                pltpu.SemaphoreType.DMA((SHARDS,)),
                pltpu.SemaphoreType.DMA((2, TILES, groups, 4)),
                pltpu.SemaphoreType.DMA((2, TILES, groups)),
            ],
            compiler_params=pltpu.CompilerParams(
                collective_id=start, has_side_effects=True, vmem_limit_bytes=40 * 1024 * 1024
            ),
        )

    operands = (
        self_query, self_key, self_value, cross_query, text_key, text_value,
        query_gain, key_gain, cross_gain, text_gain,
        jnp.asarray(cosine), jnp.asarray(sine), tile_item, row_count, text_len,
    )
    full = tile_item[SPAN - 1 :] == tile_item[: TILES - SPAN + 1]
    start = jnp.argmax(full).astype(jnp.int32)
    return lax.switch(start, [call(s) for s in range(TILES - SPAN + 1)], *operands)


def solution(mesh):
    in_specs = (
        P("tile", "head"),
        P("tile", "head"),
        P("tile", "head"),
        P("tile", "head"),
        P("tile", "head"),
        P("tile", "head"),
        P("head"),
        P("head"),
        P("head"),
        P("head"),
        P(),
        P(),
        P(),
    )
    out_specs = P("tile", "head")
    small = mesh.shape["tile"] == TILES and mesh.shape["head"] == SHARDS
    return jax.shard_map(
        fused if small else per_device, mesh=mesh, in_specs=in_specs, out_specs=out_specs, check_vma=False
    )
```
